32 devices in a mesh: seq: 16 (over z, y, core), head: 2 (over x).
Axes of the slice: x: 2, y: 2, z: 4, core: 2. Of those that a mesh axis runs over, the one named last changes fastest.
Arguments:
- queries: bfloat16 [192, 64, 128], P('seq', 'head'), may hold values from -88 to 88
- prompt_keys: bfloat16 [32768, 8, 128], P('seq', 'head'), may hold values from -4 to 4
- prompt_values: bfloat16 [32768, 8, 128], P('seq', 'head'), may hold values from -6 to 6
- suffix_keys: bfloat16 [192, 8, 1024, 128], P('seq', 'head'), may hold values from -8 to 8
- suffix_values: bfloat16 [192, 8, 1024, 128], P('seq', 'head'), may hold values from -6 to 6
- suffix_lengths: int32 [192], P('seq'), may hold values from 1 to 1024, as said below
- slot_of_sample: int32 [192], replicated, may hold values from 0 to 191, each once
- out_weight: bfloat16 [8192, 5120], P('head', 'seq'), may hold values from -0.0625 to 0.0625
Outputs:
- projected: float32 [192, 5120], P('head', 'seq')
The draws below stay inside these ranges and needn't reach their ends.
Inputs may be any that keep to these rules, and one draw needn't show every extreme that they name: `suffix_lengths`: slot j is held with the samples of seq index j // 12; some slot has exactly 1024 live tokens. `slot_of_sample`: each slot is named once.
All inputs are finite; a program needn't handle non-finite values.
Results may differ from the reference program's by a relative error of at most 0.006.
Values may be sent and summed in bfloat16 or wider, within the bound.
A program may use at most 128 MiB of HBM per device.

```python
import math
import jax
import jax.numpy as jnp
from jax import lax

HEADS = 64
KV_HEADS = 8
HEAD_DIM = 128
D = 5120
SUFFIX = 1024
PROMPT = 32768
SAMPLES = 192


def draw_queries(key, part):
    key = jax.random.fold_in(key, 1)
    base = jnp.clip(3.0 * jax.random.normal(key, (SAMPLES, HEADS, HEAD_DIM), jnp.float32), -12.0, 12.0)
    return base.astype(jnp.bfloat16)


def draw_prompt_keys(key, part):
    key = jax.random.fold_in(key, 2)
    base = jnp.clip(jax.random.normal(key, (PROMPT, KV_HEADS, HEAD_DIM), jnp.float32), -4.0, 4.0)
    return base.astype(jnp.bfloat16)


def draw_suffix_lengths(key, part):
    key = jax.random.fold_in(key, 3)
    first_key, second_key = jax.random.split(key)
    lengths = jax.random.randint(first_key, (SAMPLES,), 1, SUFFIX + 1, jnp.int32)
    picked = jax.random.randint(second_key, (), 0, SAMPLES, jnp.int32)
    return lengths.at[picked].set(SUFFIX)


def levels(stream_key, dims, pieces, least, high):
    level, own = 1.0, jax.random.fold_in(stream_key, 6)
    for dim, shards_of in pieces:
        steps = jnp.exp(jax.random.uniform(jax.random.fold_in(own, dim), (shards_of,), jnp.float32, least / len(pieces), high / len(pieces)))
        level = level * jnp.repeat(steps, dims[dim] // shards_of).reshape([-1 if axis == dim else 1 for axis in range(len(dims))])
    return level


def centred(key, extent, spread, reach, cuts=(), dtype=jnp.bfloat16):
    drawn = spread * jax.random.normal(key, extent, jnp.float32)
    if cuts:
        drawn = drawn * levels(key, extent, cuts, -0.22, 0.18)
    return jnp.clip(drawn, -reach, reach).astype(dtype)


def setup_inputs(seed: int = 0) -> dict:
    streams_of = jax.random.split(jax.random.key(seed), 9)
    return {
        "queries": draw_queries(jax.random.fold_in(streams_of[8], 71), 0),
        "prompt_keys": draw_prompt_keys(jax.random.fold_in(streams_of[8], 71), 0),
        "prompt_values": centred(streams_of[2], (PROMPT, KV_HEADS, HEAD_DIM), 1.0, 6.0, ((0, 16), (1, 2))),
        "suffix_keys": centred(streams_of[3], (SAMPLES, KV_HEADS, SUFFIX, HEAD_DIM), 1.4, 8.0, ((0, 16), (1, 2))),
        "suffix_values": centred(streams_of[4], (SAMPLES, KV_HEADS, SUFFIX, HEAD_DIM), 1.0, 6.0, ((0, 16), (1, 2))),
        "suffix_lengths": draw_suffix_lengths(jax.random.fold_in(streams_of[8], 71), 0),
        "slot_of_sample": jax.random.permutation(streams_of[6], SAMPLES).astype(jnp.int32),
        "out_weight": centred(streams_of[7], (HEADS * HEAD_DIM, D), (HEADS * HEAD_DIM) ** -0.5, 0.0625, ((0, 2), (1, 16))),
    }


def reference(queries, prompt_keys, prompt_values, suffix_keys, suffix_values, suffix_lengths, slot_of_sample, out_weight):
    total_rows = queries.shape[0]
    block_rows = math.gcd(total_rows, 8)
    group_size = HEADS // KV_HEADS
    score_scale = 1.0 / math.sqrt(HEAD_DIM)
    keys_full = prompt_keys.astype(jnp.float32)
    values_full = prompt_values.astype(jnp.float32)
    prompt_count = prompt_keys.shape[0]

    def one_block(start_row):
        first = start_row.astype(jnp.int32)
        query_block = lax.dynamic_slice_in_dim(queries, first, block_rows, 0).astype(jnp.float32)
        query_block = query_block.reshape(block_rows, KV_HEADS, group_size, HEAD_DIM)
        slots = lax.dynamic_slice_in_dim(slot_of_sample, first, block_rows, 0).astype(jnp.int32)
        tail_keys = suffix_keys[slots].astype(jnp.float32)
        tail_values = suffix_values[slots].astype(jnp.float32)
        lengths = suffix_lengths[slots]
        head_scores = jnp.einsum('bkgd,pkd->bkgp', query_block, keys_full) * score_scale
        tail_scores = jnp.einsum('bkgd,bksd->bkgs', query_block, tail_keys) * score_scale
        positions = jnp.arange(SUFFIX).astype(jnp.int32)
        live_mask = positions[None, None, None, :] < lengths.astype(jnp.int32)[:, None, None, None]
        tail_scores = jnp.where(live_mask, tail_scores, jnp.float32(-1e+30))
        scores = jnp.concatenate([head_scores, tail_scores], axis=-1)
        row_max = lax.optimization_barrier(jnp.max(scores, axis=-1, keepdims=True))
        weights = jnp.exp(scores - row_max)
        row_total = lax.optimization_barrier(jnp.sum(weights, axis=-1))
        rounded = lax.optimization_barrier(weights.astype(jnp.bfloat16)).astype(jnp.float32)
        output = jnp.einsum('bkgp,pkd->bkgd', rounded[..., :prompt_count], values_full)
        output = output + jnp.einsum('bkgs,bksd->bkgd', rounded[..., prompt_count:], tail_values)
        attention = (output / row_total[..., None]).astype(jnp.bfloat16)
        return attention.reshape(block_rows, HEADS * HEAD_DIM)
    starts = jnp.arange(0, total_rows, block_rows).astype(jnp.int32)
    attention = lax.map(one_block, starts).reshape(total_rows, HEADS * HEAD_DIM)
    return jnp.dot(attention, out_weight, preferred_element_type=jnp.float32)
```

```python
import functools
import math

import jax
import jax.numpy as jnp
from jax import lax
from jax.experimental import pallas as pl
from jax.experimental.pallas import tpu as pltpu
from jax.sharding import PartitionSpec as P

MESH = pl.DeviceIdType.MESH
NT = (((1,), (1,)), ((), ()))
TN = (((0,), (0,)), ((), ()))
NN = (((1,), (0,)), ((), ()))
LOW = -1e30
ZS, YS, CS = 4, 2, 2


def dot(a, b, dims):
    return lax.dot_general(a, b, dims, preferred_element_type=jnp.float32)


def merge(parts, unit):
    top = functools.reduce(jnp.maximum, [part[1] for part in parts])
    out, total = None, None
    for part_out, part_top, part_total in parts:
        factor = jnp.exp2((part_top - top) * unit)
        scaled, count = part_out * factor, part_total * factor
        out = scaled if out is None else out + scaled
        total = count if total is None else total + count
    return out, top, total


def kernel(
    unit,
    q_in,
    keys_in,
    values_in,
    tail_keys_in,
    tail_values_in,
    lengths,
    column_key,
    perm,
    weight_in,
    out,
    q_all,
    keys,
    values,
    tail_keys,
    tail_values,
    weight,
    own_q,
    tail_rows,
    tail_m,
    tail_l,
    tail_out,
    tail_stat,
    part,
    stat,
    core_part,
    core_stat,
    y_own,
    y_send,
    y_part,
    y_own_stat,
    y_send_stat,
    y_stat,
    z_send,
    z_send_stat,
    z_part,
    z_stat,
    att,
    total,
    x_part,
    load_sem,
    tail_sem,
    q_sems,
    qz_send_sem,
    qz_recv_sem,
    core_sems,
    y_sems,
    zs_send,
    zs_recv,
    zo_sems,
    az_send,
    az_recv,
    a_sems,
    x_sems,
):
    kv_count, rows_local, width = q_in.shape
    slots = lengths.shape[0]
    group = rows_local // slots
    chunk = YS * CS * rows_local
    tail_len = tail_keys.shape[2]
    seq, head = lax.axis_index("seq"), lax.axis_index("head")
    z, y, core = seq // (YS * CS), (seq // CS) % YS, seq % CS
    other_y, other_core, other_head = 1 - y, 1 - core, 1 - head

    def at(z_to, y_to, core_to):
        return ((z_to * YS + y_to) * CS + core_to, head)

    z_peers = [at((z + step) % ZS, y, core) for step in range(1, ZS)]
    y_peer, core_peer, x_peer = at(z, other_y, core), at(z, y, other_core), (seq, other_head)
    order = [(3 * turn) % kv_count for turn in range(kv_count)]

    def remote(source, target, send, recv, device):
        return pltpu.make_async_remote_copy(
            src_ref=source, dst_ref=target, send_sem=send, recv_sem=recv, device_id=device, device_id_type=MESH
        )

    loads = [
        pltpu.make_async_copy(keys_in, keys, load_sem.at[0]),
        pltpu.make_async_copy(values_in, values, load_sem.at[1]),
        pltpu.make_async_copy(weight_in, weight, load_sem.at[2]),
    ]

    def tail_loads(k):
        return [
            pltpu.make_async_copy(tail_keys_in.at[:, k], tail_keys.at[k], tail_sem.at[k, 0]),
            pltpu.make_async_copy(tail_values_in.at[:, k], tail_values.at[k], tail_sem.at[k, 1]),
        ]

    loads[0].start()
    loads[1].start()
    for k in order:
        for load in tail_loads(k):
            load.start()
    loads[2].start()

    barrier = pltpu.get_barrier_semaphore()
    peers = z_peers + [y_peer, core_peer, x_peer]
    for peer in peers:
        pl.semaphore_signal(barrier, inc=1, device_id=peer, device_id_type=MESH)
    pl.semaphore_wait(barrier, len(peers))

    def q_z(k):
        return [
            remote(q_in.at[k], q_all.at[k, z, y, core], qz_send_sem.at[k, i], qz_recv_sem.at[k, i], z_peers[i])
            for i in range(ZS - 1)
        ]

    def q_y(k):
        mine = q_all.at[k, :, y, core]
        return remote(mine, mine, q_sems.at[k, 0], q_sems.at[k, 1], y_peer)

    def q_core(k):
        mine = q_all.at[k, :, :, core]
        return remote(mine, mine, q_sems.at[k, 2], q_sems.at[k, 3], core_peer)

    for k in order:
        for copy in q_z(k):
            copy.start()
    for k in order:
        q_all[k, z, y, core] = q_in[k]

    def q_after_z(k):
        for copy in q_z(k):
            copy.wait()
        q_y(k).start()

    def q_after_y(k):
        q_y(k).wait()
        q_core(k).start()

    def q_ready(k):
        q_core(k).wait()

    def tail(k):
        for load in tail_loads(k):
            load.wait()
        columns = column_key.shape[1]
        row_key = seq * rows_local + lax.broadcasted_iota(jnp.int32, (rows_local, columns), 0)
        match = column_key[...] == row_key
        pick = jnp.where(match, 1.0, 0.0).astype(jnp.bfloat16)
        every = q_all[k].reshape(columns, width)
        own_q[...] = dot(pick, every, NN)

        def one(t, carry):
            rows = pl.ds(pl.multiple_of(t * group, group), group)
            scores = dot(own_q[rows, :].astype(jnp.bfloat16), tail_keys[k, t], NT)
            position = lax.broadcasted_iota(jnp.int32, scores.shape, 1)
            scores = jnp.where(position < lengths[t], scores, LOW)
            top = jnp.max(scores, axis=1, keepdims=True)
            weights = jnp.exp2((scores - top) * unit)
            tail_rows[rows, :] = dot(weights.astype(jnp.bfloat16), tail_values[k, t], NN)
            tail_m[rows, :] = jnp.broadcast_to(top, (group, width))
            tail_l[rows, :] = jnp.broadcast_to(jnp.sum(weights, axis=1, keepdims=True), (group, width))
            return carry

        lax.fori_loop(0, slots, one, 0, unroll=4)
        for c in range(columns // chunk):
            span = slice(c * chunk, (c + 1) * chunk)
            here = column_key[:, span] == row_key[:, span]
            tail_out[c] = dot(tail_rows[...].astype(jnp.bfloat16), jnp.where(here, 1.0, 0.0).astype(jnp.bfloat16), TN)
            top = jnp.max(jnp.where(here, tail_m[:, :1], LOW), axis=0, keepdims=True)
            count = jnp.sum(jnp.where(here, tail_l[:, :1], 0.0), axis=0, keepdims=True)
            tail_stat[c, 0:1] = top
            tail_stat[c, 1:2] = count

    def prompt(k, pair):
        q = q_all[k, pl.ds(pair * 2, 2)].reshape(2 * chunk, width)
        scores = dot(keys[k], q, NT)
        top = jnp.max(scores, axis=0, keepdims=True)
        weights = jnp.exp2((scores - top) * unit)
        count = jnp.sum(weights, axis=0, keepdims=True)
        rows = dot(values[k], weights.astype(jnp.bfloat16), NN)
        for c in range(2):
            span = slice(c * chunk, (c + 1) * chunk)
            at_chunk = pair * 2 + c
            o, m, l = merge(
                [
                    (rows[:, span], top[:, span], count[:, span]),
                    (tail_out[at_chunk], tail_stat[at_chunk, 0:1], tail_stat[at_chunk, 1:2]),
                ],
                unit,
            )
            part[k, pair, c] = o.astype(jnp.bfloat16)
            stat[k, pair, c, 0:1] = m
            stat[k, pair, c, 1:2] = l

    def sum_core(k):
        return [
            remote(part.at[k, :, other_core], core_part.at[k], core_sems.at[k, 0], core_sems.at[k, 1], core_peer),
            remote(stat.at[k, :, other_core], core_stat.at[k], core_sems.at[k, 2], core_sems.at[k, 3], core_peer),
        ]

    def sum_y(k):
        return [
            remote(y_send.at[k], y_part.at[k], y_sems.at[k, 0], y_sems.at[k, 1], y_peer),
            remote(y_send_stat.at[k], y_stat.at[k], y_sems.at[k, 2], y_sems.at[k, 3], y_peer),
        ]

    def sum_z(k):
        slot = (z - k + ZS - 1) % ZS
        return [
            remote(z_send.at[k], z_part.at[slot], zs_send.at[k, 0], zs_recv.at[slot, 0], at(k, y, core)),
            remote(z_send_stat.at[k], z_stat.at[slot], zs_send.at[k, 1], zs_recv.at[slot, 1], at(k, y, core)),
        ]

    def att_z(k):
        mine = att.at[k, y, core]
        return [
            remote(mine, mine, az_send.at[i], az_recv.at[k], at((k + 1 + i) % ZS, y, core)) for i in range(ZS - 1)
        ]

    def att_y(k):
        mine = att.at[k, y, core]
        return remote(mine, mine, a_sems.at[k, 0], a_sems.at[k, 1], y_peer)

    def att_core(k):
        mine = att.at[k, :, core]
        return remote(mine, mine, a_sems.at[k, 2], a_sems.at[k, 3], core_peer)

    def step_a(k):
        for copy in sum_core(k):
            copy.start()

    def step_b(k):
        for copy in sum_core(k):
            copy.wait()

        def joined(i):
            return merge(
                [
                    (part[k, i, core].astype(jnp.float32), stat[k, i, core, 0:1], stat[k, i, core, 1:2]),
                    (core_part[k, i].astype(jnp.float32), core_stat[k, i, 0:1], core_stat[k, i, 1:2]),
                ],
                unit,
            )

        o, m, l = joined(other_y)
        y_send[k] = o.astype(jnp.bfloat16)
        y_send_stat[k, 0:1] = m
        y_send_stat[k, 1:2] = l
        for copy in sum_y(k):
            copy.start()
        o, m, l = joined(y)
        y_own[k] = o
        y_own_stat[k, 0:1] = m
        y_own_stat[k, 1:2] = l

    def step_c(k):
        for copy in sum_y(k):
            copy.wait()
        o, m, l = merge(
            [
                (y_own[k], y_own_stat[k, 0:1], y_own_stat[k, 1:2]),
                (y_part[k].astype(jnp.float32), y_stat[k, 0:1], y_stat[k, 1:2]),
            ],
            unit,
        )
        y_own[k] = o
        z_send[k] = o.astype(jnp.bfloat16)
        z_send_stat[k, 0:1] = m
        z_send_stat[k, 1:2] = l

        @pl.when(z != k)
        def _():
            for copy in sum_z(k):
                copy.start()

    def step_d(k):
        @pl.when(z != k)
        def _():
            for copy in sum_z(k):
                copy.wait_send()

        @pl.when(z == k)
        def _():
            parts = [(y_own[k], z_send_stat[k, 0:1], z_send_stat[k, 1:2])]
            for slot in range(ZS - 1):
                device = at(k, y, core)
                remote(z_send.at[k], z_part.at[slot], zs_send.at[k, 0], zs_recv.at[slot, 0], device).wait_recv()
                remote(z_send_stat.at[k], z_stat.at[slot], zs_send.at[k, 1], zs_recv.at[slot, 1], device).wait_recv()
                parts.append((z_part[slot].astype(jnp.float32), z_stat[slot, 0:1], z_stat[slot, 1:2]))
            o, _, l = merge(parts, unit)
            attention = (o / l).astype(jnp.bfloat16)
            rows = dot(perm[...], attention, NT).astype(jnp.bfloat16)
            att[k, y, core] = rows.reshape(att.shape[3:])
            for copy in att_z(k):
                copy.start()

    def step_e(k):
        @pl.when(z != k)
        def _():
            att_z(k)[0].wait_recv()

        att_y(k).start()

    def step_f(k):
        @pl.when(z == k)
        def _():
            for copy in att_z(k):
                copy.wait_send()

        att_y(k).wait()
        att_core(k).start()

    def step_g(k):
        att_core(k).wait()
        value = None
        for g in range(0, group, 2):
            block = jnp.concatenate(
                [
                    jnp.concatenate([att[k, i, j, g + h] for i in range(YS) for j in range(CS)], axis=0)
                    for h in range(2)
                ],
                axis=1,
            )
            first = (k * group + g) * width
            term = dot(block, weight[first : first + 2 * width, :], NN)
            value = term if value is None else value + term
        return value

    a, b, c, d = order
    q_after_z(a)
    q_after_z(b)
    q_after_y(a)
    loads[0].wait()
    loads[1].wait()
    q_ready(a)

    hooks = {
        0: [(q_after_z, c), (q_after_y, b)],
        1: [(step_a, a), (q_after_z, d), (q_after_y, c), (q_ready, b)],
        2: [(step_b, a), (q_after_y, d)],
        3: [(step_c, a), (step_a, b), (q_ready, c)],
        4: [(step_d, a), (step_b, b)],
        5: [(step_e, a), (step_c, b), (step_a, c), (q_ready, d)],
        6: [(step_f, a), (step_d, b), (step_b, c)],
        7: [(step_a, d), (step_e, b), (step_c, c)],
    }

    def turn(i, carry):
        k, pair = (3 * (i // 2)) % kv_count, i % 2

        @pl.when(pair == 0)
        def _():
            tail(k)

        prompt(k, pair)
        for at_turn, calls in hooks.items():

            @pl.when(i == at_turn)
            def _(calls=calls):
                for call, at_k in calls:
                    call(at_k)

        return carry

    lax.fori_loop(0, 2 * kv_count, turn, 0)
    step_b(d)
    step_d(c)
    step_f(b)
    step_c(d)
    loads[2].wait()
    value = step_g(a)
    step_e(c)
    step_d(d)
    value += step_g(b)
    step_f(c)
    step_e(d)
    value += step_g(c)
    step_f(d)
    value += step_g(d)
    half = value.shape[0] // 2
    total[0] = value[:half]
    total[1] = value[half:]
    swap = remote(total.at[other_head], x_part, x_sems.at[0], x_sems.at[1], x_peer)
    swap.start()
    swap.wait()
    out[...] = total[head] + x_part[...]


def fused(queries, prompt_keys, prompt_values, suffix_keys, suffix_values, suffix_lengths, slot_of_sample, out_weight):
    slots, heads, width = queries.shape
    kv = prompt_keys.shape[1]
    group = heads // kv
    rows = slots * group
    positions = prompt_keys.shape[0]
    samples = slot_of_sample.shape[0]
    columns = samples * group
    chunk = YS * CS * rows
    share = chunk // group
    tail_len = suffix_keys.shape[2]
    half, out_columns = samples // 2, out_weight.shape[1]
    unit = math.log2(math.e) / math.sqrt(width)

    q = queries.reshape(slots, kv, group, width).transpose(1, 0, 2, 3).reshape(kv, rows, width)
    keys = prompt_keys.transpose(1, 0, 2)
    values = prompt_values.transpose(1, 2, 0)
    column_key = (slot_of_sample[:, None] * group + jnp.arange(group, dtype=jnp.int32)).reshape(1, columns)
    place = jnp.arange(chunk, dtype=jnp.int32)
    perm = (((place % share) * group + place // share)[:, None] == place[None, :]).astype(jnp.bfloat16)

    bf16, f32 = jnp.bfloat16, jnp.float32
    vmem, hbm = pl.BlockSpec(memory_space=pltpu.VMEM), pl.BlockSpec(memory_space=pl.ANY)
    sem = pltpu.SemaphoreType.DMA
    return pl.pallas_call(
        functools.partial(kernel, unit),
        out_shape=jax.ShapeDtypeStruct((half, out_columns), f32),
        in_specs=[vmem, hbm, hbm, hbm, hbm, pl.BlockSpec(memory_space=pltpu.SMEM), vmem, vmem, hbm],
        out_specs=vmem,
        scratch_shapes=[
            pltpu.VMEM((kv, ZS, YS, CS, rows, width), bf16),
            pltpu.VMEM(keys.shape, bf16),
            pltpu.VMEM(values.shape, bf16),
            pltpu.VMEM((kv, slots, tail_len, width), bf16),
            pltpu.VMEM((kv, slots, tail_len, width), bf16),
            pltpu.VMEM(out_weight.shape, bf16),
            pltpu.VMEM((rows, width), f32),
            pltpu.VMEM((rows, width), f32),
            pltpu.VMEM((rows, width), f32),
            pltpu.VMEM((rows, width), f32),
            pltpu.VMEM((ZS, width, chunk), f32),
            pltpu.VMEM((ZS, 8, chunk), f32),
            pltpu.VMEM((kv, YS, CS, width, chunk), bf16),
            pltpu.VMEM((kv, YS, CS, 8, chunk), f32),
            pltpu.VMEM((kv, YS, width, chunk), bf16),
            pltpu.VMEM((kv, YS, 8, chunk), f32),
            pltpu.VMEM((kv, width, chunk), f32),
            pltpu.VMEM((kv, width, chunk), bf16),
            pltpu.VMEM((kv, width, chunk), bf16),
            pltpu.VMEM((kv, 8, chunk), f32),
            pltpu.VMEM((kv, 8, chunk), f32),
            pltpu.VMEM((kv, 8, chunk), f32),
            pltpu.VMEM((kv, width, chunk), bf16),
            pltpu.VMEM((kv, 8, chunk), f32),
            pltpu.VMEM((ZS - 1, width, chunk), bf16),
            pltpu.VMEM((ZS - 1, 8, chunk), f32),
            pltpu.VMEM((kv, YS, CS, group, share, width), bf16),
            pltpu.VMEM((2, half, out_columns), f32),
            pltpu.VMEM((half, out_columns), f32),
            sem((3,)),
            sem((kv, 2)),
            sem((kv, 4)),
            sem((kv, ZS - 1)),
            sem((kv, ZS - 1)),
            sem((kv, 4)),
            sem((kv, 4)),
            sem((kv, 2)),
            sem((ZS - 1, 2)),
            sem((1,)),
            sem((ZS - 1,)),
            sem((kv,)),
            sem((kv, 4)),
            sem((2,)),
        ],
        compiler_params=pltpu.CompilerParams(
            collective_id=0, has_side_effects=True, vmem_limit_bytes=62 * 1024 * 1024
        ),
    )(q, keys, values, suffix_keys, suffix_values, suffix_lengths, column_key, perm, out_weight)


def partial_softmax(scores, values_block, equation):
    row_max = jnp.max(scores, axis=-1)
    weights = jnp.exp(scores - row_max[..., None])
    row_total = jnp.sum(weights, axis=-1)
    output = jnp.einsum(
        equation, weights.astype(jnp.bfloat16), values_block, preferred_element_type=jnp.float32
    )
    return (output, row_max, row_total)


def per_device(
    queries,
    prompt_keys,
    prompt_values,
    suffix_keys,
    suffix_values,
    suffix_lengths,
    slot_of_sample,
    out_weight,
):
    local_count, heads_local, head_width = queries.shape
    kv_local = prompt_keys.shape[1]
    group_size = heads_local // kv_local
    score_scale = 1.0 / math.sqrt(head_width)
    all_queries = lax.all_gather(queries, "seq", axis=0, tiled=True)
    total_rows = all_queries.shape[0]
    block_rows = math.gcd(total_rows, 64)

    def prefix_block(query_block):
        grouped = query_block.reshape(block_rows, kv_local, group_size, head_width)
        scores = (
            jnp.einsum("bkgd,pkd->bkgp", grouped, prompt_keys, preferred_element_type=jnp.float32)
            * score_scale
        )
        output, row_max, row_total = partial_softmax(scores, prompt_values, "bkgp,pkd->bkgd")
        return (
            output.reshape(block_rows, heads_local, head_width),
            row_max.reshape(block_rows, heads_local),
            row_total.reshape(block_rows, heads_local),
        )

    blocks = all_queries.reshape(total_rows // block_rows, block_rows, heads_local, head_width)
    pre_out, pre_max, pre_total = lax.map(prefix_block, blocks)
    pre_out = pre_out.reshape(total_rows, heads_local, head_width)
    pre_max = pre_max.reshape(total_rows, heads_local)
    pre_total = pre_total.reshape(total_rows, heads_local)
    my_slots = lax.axis_index("seq") * local_count + jnp.arange(local_count, dtype=jnp.int32)
    matches = (slot_of_sample[None, :] == my_slots[:, None]).astype(jnp.int32)
    samples = jnp.sum(matches * jnp.arange(total_rows, dtype=jnp.int32)[None, :], axis=1)
    own_queries = all_queries[samples].reshape(local_count, kv_local, group_size, head_width)
    tail_scores = (
        jnp.einsum("bkgd,bksd->bkgs", own_queries, suffix_keys, preferred_element_type=jnp.float32)
        * score_scale
    )
    positions = jnp.arange(suffix_keys.shape[2], dtype=jnp.int32)
    live_mask = positions[None, None, None, :] < suffix_lengths[:, None, None, None]
    tail_scores = jnp.where(live_mask, tail_scores, jnp.float32(-1e30))
    tail_out, tail_max, tail_total = partial_softmax(tail_scores, suffix_values, "bkgs,bksd->bkgd")
    tail_out = tail_out.reshape(local_count, heads_local, head_width)
    tail_max = tail_max.reshape(local_count, heads_local)
    tail_total = tail_total.reshape(local_count, heads_local)
    old_max = pre_max[samples]
    joint_max = jnp.maximum(old_max, tail_max)
    old_factor = jnp.exp(old_max - joint_max)
    new_factor = jnp.exp(tail_max - joint_max)
    joint_out = pre_out[samples] * old_factor[..., None] + tail_out * new_factor[..., None]
    joint_total = pre_total[samples] * old_factor + tail_total * new_factor
    pre_out = pre_out.at[samples].set(joint_out)
    pre_max = pre_max.at[samples].set(joint_max)
    pre_total = pre_total.at[samples].set(joint_total)
    got_out, got_max, got_total = (
        lax.all_to_all(pre_out[None], "seq", split_axis=1, concat_axis=0, tiled=True),
        lax.all_to_all(pre_max[None], "seq", split_axis=1, concat_axis=0, tiled=True),
        lax.all_to_all(pre_total[None], "seq", split_axis=1, concat_axis=0, tiled=True),
    )
    best = jnp.max(got_max, axis=0)
    factors = jnp.exp(got_max - best[None])
    merged_out = jnp.sum(got_out * factors[..., None], axis=0)
    merged_total = jnp.sum(got_total * factors, axis=0)
    attention = (merged_out / merged_total[..., None]).astype(jnp.bfloat16)
    attention = attention.reshape(local_count, heads_local * head_width)
    terms = jnp.dot(
        lax.all_gather(attention, "seq", axis=0, tiled=True),
        out_weight,
        preferred_element_type=jnp.float32,
    )
    return lax.psum_scatter(terms, "head", scatter_dimension=0, tiled=True)


def solution(mesh):
    placed = (
        P("seq", "head", None),
        P("seq", "head", None),
        P("seq", "head", None),
        P("seq", "head", None, None),
        P("seq", "head", None, None),
        P("seq"),
        P(),
        P("head", "seq"),
    )

    def body(*arrays):
        kv = arrays[1].shape[1]
        fits = mesh.shape["seq"] == ZS * YS * CS and mesh.shape["head"] == 2 and kv == ZS
        return (fused if fits else per_device)(*arrays)

    return jax.shard_map(body, mesh=mesh, in_specs=placed, out_specs=P("head", "seq"), check_vma=False)
```

```python
import functools
import math

import jax
import jax.numpy as jnp
from jax import lax
from jax.experimental import pallas as pl
from jax.experimental.pallas import tpu as pltpu
from jax.sharding import PartitionSpec as P

MESH = pl.DeviceIdType.MESH
NT = (((1,), (1,)), ((), ()))
TN = (((0,), (0,)), ((), ()))
NN = (((1,), (0,)), ((), ()))
LOW = -1e30
ZS, YS, CS = 4, 2, 2


def dot(a, b, dims):
    return lax.dot_general(a, b, dims, preferred_element_type=jnp.float32)


def merge(parts, unit):
    top = functools.reduce(jnp.maximum, [part[1] for part in parts])
    out, total = None, None
    for part_out, part_top, part_total in parts:
        factor = jnp.exp2((part_top - top) * unit)
        scaled, count = part_out * factor, part_total * factor
        out = scaled if out is None else out + scaled
        total = count if total is None else total + count
    return out, top, total


def kernel(
    unit,
    q_in,
    keys_in,
    values_in,
    tail_keys_in,
    tail_values_in,
    lengths,
    slot_of,
    weight_in,
    out,
    q_own,
    raw_keys,
    raw_values,
    perm,
    match,
    q_all,
    keys,
    values,
    tail_keys,
    tail_values,
    weight,
    own_q,
    tail_scores,
    tail_rows,
    tail_out,
    tail_stat,
    part,
    stat,
    core_part,
    core_stat,
    y_own,
    y_send,
    y_part,
    y_own_stat,
    y_send_stat,
    y_stat,
    z_send,
    z_send_stat,
    z_part,
    z_stat,
    att,
    total,
    x_part,
    load_sem,
    tail_sem,
    q_sems,
    qz_send_sem,
    qz_recv_sem,
    core_sems,
    y_sems,
    zs_send,
    zs_recv,
    zo_sems,
    az_send,
    az_recv,
    a_sems,
    x_sems,
):
    kv_count, rows_local, width = q_own.shape
    slots = lengths.shape[0]
    group = rows_local // slots
    samples = slot_of.shape[1]
    chunk = YS * CS * rows_local
    seq, head = lax.axis_index("seq"), lax.axis_index("head")
    z, y, core = seq // (YS * CS), (seq // CS) % YS, seq % CS
    other_y, other_core, other_head = 1 - y, 1 - core, 1 - head

    def at(z_to, y_to, core_to):
        return ((z_to * YS + y_to) * CS + core_to, head)

    z_peers = [at((z + step) % ZS, y, core) for step in range(1, ZS)]
    y_peer, core_peer, x_peer = at(z, other_y, core), at(z, y, other_core), (seq, other_head)
    order = [(3 * turn) % kv_count for turn in range(kv_count)]

    def remote(source, target, send, recv, device):
        return pltpu.make_async_remote_copy(
            src_ref=source, dst_ref=target, send_sem=send, recv_sem=recv, device_id=device, device_id_type=MESH
        )

    loads = [
        pltpu.make_async_copy(keys_in, raw_keys, load_sem.at[0]),
        pltpu.make_async_copy(values_in, raw_values, load_sem.at[1]),
        pltpu.make_async_copy(weight_in, weight, load_sem.at[2]),
    ]

    def tail_loads(k):
        return [
            pltpu.make_async_copy(tail_keys_in.at[:, k], tail_keys.at[k], tail_sem.at[k, 0]),
            pltpu.make_async_copy(tail_values_in.at[:, k], tail_values.at[k], tail_sem.at[k, 1]),
        ]

    loads[0].start()
    loads[1].start()
    for k in order:
        for load in tail_loads(k):
            load.start()
    loads[2].start()

    def grid(shape, axis):
        return lax.broadcasted_iota(jnp.int32, shape, axis)

    def onehot(chosen):
        return jnp.where(chosen, 1.0, 0.0).astype(jnp.bfloat16)

    flat = q_in[...].reshape(-1, width)
    shape = (rows_local, flat.shape[0])
    place = (grid(shape, 0) // group) * (kv_count * group) + grid(shape, 0) % group
    for k in order:
        q_own[k] = dot(onehot(grid(shape, 1) == place + k * group), flat, NN).astype(jnp.bfloat16)

    barrier = pltpu.get_barrier_semaphore()
    peers = z_peers + [y_peer, core_peer, x_peer]
    for peer in peers:
        pl.semaphore_signal(barrier, inc=1, device_id=peer, device_id_type=MESH)
    pl.semaphore_wait(barrier, len(peers))

    def q_z(k):
        return [
            remote(q_own.at[k], q_all.at[k, z, y, core], qz_send_sem.at[k, i], qz_recv_sem.at[k, i], z_peers[i])
            for i in range(ZS - 1)
        ]

    def q_y(k):
        mine = q_all.at[k, :, y, core]
        return remote(mine, mine, q_sems.at[k, 0], q_sems.at[k, 1], y_peer)

    def q_core(k):
        mine = q_all.at[k, :, :, core]
        return remote(mine, mine, q_sems.at[k, 2], q_sems.at[k, 3], core_peer)

    for k in order:
        for copy in q_z(k):
            copy.start()
    for k in order:
        q_all[k, z, y, core] = q_own[k]

    def q_after_z(k):
        for copy in q_z(k):
            copy.wait()
        q_y(k).start()

    def q_after_y(k):
        q_y(k).wait()
        q_core(k).start()

    def q_ready(k):
        q_core(k).wait()

    def split_keys():
        size = 256 // kv_count
        shape = (256, 256)
        pick = onehot(grid(shape, 1) == (grid(shape, 0) % size) * kv_count + grid(shape, 0) // size)

        def one(i, carry):
            rows = raw_keys[pl.ds(pl.multiple_of(i * 256, 256), 256), :]
            apart = dot(pick, rows, NN).astype(jnp.bfloat16)
            for k in range(kv_count):
                keys[k, pl.ds(pl.multiple_of(i * size, size), size), :] = apart[k * size : (k + 1) * size]
            return carry

        lax.fori_loop(0, raw_keys.shape[0] // 256, one, 0, unroll=4)

    def split_values():
        wide = 128 * kv_count
        shape = (wide, wide)
        pick = onehot(grid(shape, 0) == (grid(shape, 1) % 128) * kv_count + grid(shape, 1) // 128)

        def one(i, carry):
            rows = raw_values[pl.ds(pl.multiple_of(i * wide, wide), wide), :]
            apart = dot(rows, pick, TN).astype(jnp.bfloat16)
            for k in range(kv_count):
                values[k, :width, pl.ds(pl.multiple_of(i * 128, 128), 128)] = apart[:, k * 128 : (k + 1) * 128]
            return carry

        lax.fori_loop(0, raw_values.shape[0] // wide, one, 0, unroll=2)
        for k in range(kv_count):
            values[k, width:, :] = jnp.ones((values.shape[1] - width, values.shape[2]), jnp.bfloat16)

    def prepare():
        columns = samples * group
        row_slot = seq * slots + grid((rows_local, samples), 0) // group
        shape = (samples, columns)
        spread = onehot(grid(shape, 1) // group == grid(shape, 0))
        wide = dot(onehot(slot_of[...] == row_slot), spread, NN)
        shape = (rows_local, columns)
        match[...] = jnp.where(grid(shape, 1) % group == grid(shape, 0) % group, wide, 0.0).astype(jnp.bfloat16)
        shape = (group, chunk // group, chunk)
        perm[...] = onehot(grid(shape, 2) == grid(shape, 1) * group + grid(shape, 0)).reshape(chunk, chunk)

    def tail(k):
        for load in tail_loads(k):
            load.wait()
        every = q_all[k].reshape(samples * group, width)
        own_q[...] = dot(match[...], every, NN)
        for t in range(slots):
            rows = slice(t * group, (t + 1) * group)
            scores = dot(own_q[rows, :].astype(jnp.bfloat16), tail_keys[k, t], NT)
            tail_scores[rows, :] = jnp.where(grid(scores.shape, 1) < lengths[t], scores, LOW)
        scores = tail_scores[...]
        top = jnp.max(scores, axis=1, keepdims=True)
        weights = jnp.exp2((scores - top) * unit)
        count = jnp.sum(weights, axis=1, keepdims=True)
        tail_scores[...] = weights
        for t in range(slots):
            rows = slice(t * group, (t + 1) * group)
            tail_rows[rows, :] = dot(tail_scores[rows, :].astype(jnp.bfloat16), tail_values[k, t], NN)
        for c in range(samples * group // chunk):
            place = match[:, c * chunk : (c + 1) * chunk]
            here = place.astype(jnp.float32) > 0.5
            tail_out[c] = dot(tail_rows[...].astype(jnp.bfloat16), place, TN)
            tail_stat[c, 0:1] = jnp.max(jnp.where(here, top, LOW), axis=0, keepdims=True)
            tail_stat[c, 1:2] = jnp.sum(jnp.where(here, count, 0.0), axis=0, keepdims=True)

    def prompt(k, pair):
        q = q_all[k, pl.ds(pair * 2, 2)].reshape(2 * chunk, width)
        scores = dot(keys[k], q, NT)
        top = jnp.max(scores, axis=0, keepdims=True)
        weights = jnp.exp2((scores - top) * unit)
        both = dot(values[k], weights.astype(jnp.bfloat16), NN)
        rows, count = both[:width], both[width : width + 1]
        for c in range(2):
            span = slice(c * chunk, (c + 1) * chunk)
            at_chunk = pair * 2 + c
            o, m, l = merge(
                [
                    (rows[:, span], top[:, span], count[:, span]),
                    (tail_out[at_chunk], tail_stat[at_chunk, 0:1], tail_stat[at_chunk, 1:2]),
                ],
                unit,
            )
            part[k, pair, c] = o.astype(jnp.bfloat16)
            stat[k, pair, c, 0:1] = m
            stat[k, pair, c, 1:2] = l

    def sum_core(k):
        return [
            remote(part.at[k, :, other_core], core_part.at[k], core_sems.at[k, 0], core_sems.at[k, 1], core_peer),
            remote(stat.at[k, :, other_core], core_stat.at[k], core_sems.at[k, 2], core_sems.at[k, 3], core_peer),
        ]

    def sum_y(k):
        return [
            remote(y_send.at[k], y_part.at[k], y_sems.at[k, 0], y_sems.at[k, 1], y_peer),
            remote(y_send_stat.at[k], y_stat.at[k], y_sems.at[k, 2], y_sems.at[k, 3], y_peer),
        ]

    def sum_z(k):
        slot = (z - k + ZS - 1) % ZS
        return [
            remote(z_send.at[k], z_part.at[slot], zs_send.at[k, 0], zs_recv.at[slot, 0], at(k, y, core)),
            remote(z_send_stat.at[k], z_stat.at[slot], zs_send.at[k, 1], zs_recv.at[slot, 1], at(k, y, core)),
        ]

    def att_z(k):
        mine = att.at[k, y, core]
        return [
            remote(mine, mine, az_send.at[i], az_recv.at[k], at((k + 1 + i) % ZS, y, core)) for i in range(ZS - 1)
        ]

    def att_y(k):
        mine = att.at[k, y, core]
        return remote(mine, mine, a_sems.at[k, 0], a_sems.at[k, 1], y_peer)

    def att_core(k):
        mine = att.at[k, :, core]
        return remote(mine, mine, a_sems.at[k, 2], a_sems.at[k, 3], core_peer)

    def step_a(k):
        for copy in sum_core(k):
            copy.start()

    def step_b(k):
        for copy in sum_core(k):
            copy.wait()

        def joined(i):
            return merge(
                [
                    (part[k, i, core].astype(jnp.float32), stat[k, i, core, 0:1], stat[k, i, core, 1:2]),
                    (core_part[k, i].astype(jnp.float32), core_stat[k, i, 0:1], core_stat[k, i, 1:2]),
                ],
                unit,
            )

        o, m, l = joined(other_y)
        y_send[k] = o.astype(jnp.bfloat16)
        y_send_stat[k, 0:1] = m
        y_send_stat[k, 1:2] = l
        for copy in sum_y(k):
            copy.start()
        o, m, l = joined(y)
        y_own[k] = o
        y_own_stat[k, 0:1] = m
        y_own_stat[k, 1:2] = l

    def step_c(k):
        for copy in sum_y(k):
            copy.wait()
        o, m, l = merge(
            [
                (y_own[k], y_own_stat[k, 0:1], y_own_stat[k, 1:2]),
                (y_part[k].astype(jnp.float32), y_stat[k, 0:1], y_stat[k, 1:2]),
            ],
            unit,
        )
        y_own[k] = o
        z_send[k] = o.astype(jnp.bfloat16)
        z_send_stat[k, 0:1] = m
        z_send_stat[k, 1:2] = l

        @pl.when(z != k)
        def _():
            for copy in sum_z(k):
                copy.start()

    def step_d(k):
        @pl.when(z != k)
        def _():
            for copy in sum_z(k):
                copy.wait_send()

        @pl.when(z == k)
        def _():
            parts = [(y_own[k], z_send_stat[k, 0:1], z_send_stat[k, 1:2])]
            for slot in range(ZS - 1):
                device = at(k, y, core)
                remote(z_send.at[k], z_part.at[slot], zs_send.at[k, 0], zs_recv.at[slot, 0], device).wait_recv()
                remote(z_send_stat.at[k], z_stat.at[slot], zs_send.at[k, 1], zs_recv.at[slot, 1], device).wait_recv()
                parts.append((z_part[slot].astype(jnp.float32), z_stat[slot, 0:1], z_stat[slot, 1:2]))
            o, _, l = merge(parts, unit)
            attention = (o / l).astype(jnp.bfloat16)
            rows = dot(perm[...], attention, NT).astype(jnp.bfloat16)
            att[k, y, core] = rows.reshape(att.shape[3:])
            for copy in att_z(k):
                copy.start()

    def step_e(k):
        @pl.when(z != k)
        def _():
            att_z(k)[0].wait_recv()

        att_y(k).start()

    def step_f(k):
        @pl.when(z == k)
        def _():
            for copy in att_z(k):
                copy.wait_send()

        att_y(k).wait()
        att_core(k).start()

    def step_g(k):
        att_core(k).wait()
        value = None
        for g in range(0, group, 2):
            block = jnp.concatenate(
                [
                    jnp.concatenate([att[k, i, j, g + h] for i in range(YS) for j in range(CS)], axis=0)
                    for h in range(2)
                ],
                axis=1,
            )
            first = (k * group + g) * width
            term = dot(block, weight[:, first : first + 2 * width], NT)
            value = term if value is None else value + term
        return value

    a, b, c, d = order
    prepare()
    loads[0].wait()
    split_keys()
    q_after_z(a)
    loads[1].wait()
    split_values()
    q_after_y(a)
    q_after_z(b)
    q_ready(a)

    hooks = {
        0: [(q_after_z, c), (q_after_y, b)],
        1: [(step_a, a), (q_after_z, d), (q_after_y, c), (q_ready, b)],
        2: [(step_b, a), (q_after_y, d)],
        3: [(step_c, a), (step_a, b), (q_ready, c)],
        4: [(step_d, a), (step_b, b)],
        5: [(step_e, a), (step_c, b), (step_a, c), (q_ready, d)],
        6: [(step_f, a), (step_d, b), (step_b, c)],
        7: [(step_a, d), (step_e, b), (step_c, c)],
    }

    def turn(i, carry):
        k, pair = (3 * (i // 2)) % kv_count, i % 2

        @pl.when(pair == 0)
        def _():
            tail(k)

        prompt(k, pair)
        for at_turn, calls in hooks.items():

            @pl.when(i == at_turn)
            def _(calls=calls):
                for call, at_k in calls:
                    call(at_k)

        return carry

    lax.fori_loop(0, 2 * kv_count, turn, 0)
    step_b(d)
    step_d(c)
    step_f(b)
    step_c(d)
    loads[2].wait()
    value = step_g(a)
    step_e(c)
    step_d(d)
    value += step_g(b)
    step_f(c)
    step_e(d)
    value += step_g(c)
    step_f(d)
    value += step_g(d)
    half = value.shape[0] // 2
    total[0] = value[:half]
    total[1] = value[half:]
    swap = remote(total.at[other_head], x_part, x_sems.at[0], x_sems.at[1], x_peer)
    swap.start()
    swap.wait()
    out[...] = total[head] + x_part[...]


def fused(queries, prompt_keys, prompt_values, suffix_keys, suffix_values, suffix_lengths, slot_of_sample, out_weight):
    slots, heads, width = queries.shape
    kv = prompt_keys.shape[1]
    group = heads // kv
    rows = slots * group
    positions = prompt_keys.shape[0]
    samples = slot_of_sample.shape[0]
    columns = samples * group
    chunk = YS * CS * rows
    share = chunk // group
    tail_len = suffix_keys.shape[2]
    half, out_columns = samples // 2, out_weight.shape[1]
    unit = math.log2(math.e) / math.sqrt(width)

    flat_keys = prompt_keys.reshape(positions * kv, width)
    flat_values = prompt_values.reshape(positions * kv, width)

    bf16, f32 = jnp.bfloat16, jnp.float32
    vmem, hbm = pl.BlockSpec(memory_space=pltpu.VMEM), pl.BlockSpec(memory_space=pl.ANY)
    sem = pltpu.SemaphoreType.DMA
    return pl.pallas_call(
        functools.partial(kernel, unit),
        out_shape=jax.ShapeDtypeStruct((half, out_columns), f32),
        in_specs=[vmem, hbm, hbm, hbm, hbm, pl.BlockSpec(memory_space=pltpu.SMEM), vmem, hbm],
        out_specs=vmem,
        scratch_shapes=[
            pltpu.VMEM((kv, rows, width), bf16),
            pltpu.VMEM(flat_keys.shape, bf16),
            pltpu.VMEM(flat_values.shape, bf16),
            pltpu.VMEM((chunk, chunk), bf16),
            pltpu.VMEM((rows, columns), bf16),
            pltpu.VMEM((kv, ZS, YS, CS, rows, width), bf16),
            pltpu.VMEM((kv, positions, width), bf16),
            pltpu.VMEM((kv, width + 16, positions), bf16),
            pltpu.VMEM((kv, slots, tail_len, width), bf16),
            pltpu.VMEM((kv, slots, tail_len, width), bf16),
            pltpu.VMEM(out_weight.shape[::-1], bf16),
            pltpu.VMEM((rows, width), f32),
            pltpu.VMEM((rows, tail_len), f32),
            pltpu.VMEM((rows, width), f32),
            pltpu.VMEM((ZS, width, chunk), f32),
            pltpu.VMEM((ZS, 8, chunk), f32),
            pltpu.VMEM((kv, YS, CS, width, chunk), bf16),
            pltpu.VMEM((kv, YS, CS, 8, chunk), f32),
            pltpu.VMEM((kv, YS, width, chunk), bf16),
            pltpu.VMEM((kv, YS, 8, chunk), f32),
            pltpu.VMEM((kv, width, chunk), f32),
            pltpu.VMEM((kv, width, chunk), bf16),
            pltpu.VMEM((kv, width, chunk), bf16),
            pltpu.VMEM((kv, 8, chunk), f32),
            pltpu.VMEM((kv, 8, chunk), f32),
            pltpu.VMEM((kv, 8, chunk), f32),
            pltpu.VMEM((kv, width, chunk), bf16),
            pltpu.VMEM((kv, 8, chunk), f32),
            pltpu.VMEM((ZS - 1, width, chunk), bf16),
            pltpu.VMEM((ZS - 1, 8, chunk), f32),
            pltpu.VMEM((kv, YS, CS, group, share, width), bf16),
            pltpu.VMEM((2, half, out_columns), f32),
            pltpu.VMEM((half, out_columns), f32),
            sem((3,)),
            sem((kv, 2)),
            sem((kv, 4)),
            sem((kv, ZS - 1)),
            sem((kv, ZS - 1)),
            sem((kv, 4)),
            sem((kv, 4)),
            sem((kv, 2)),
            sem((ZS - 1, 2)),
            sem((1,)),
            sem((ZS - 1,)),
            sem((kv,)),
            sem((kv, 4)),
            sem((2,)),
        ],
        compiler_params=pltpu.CompilerParams(
            collective_id=0, has_side_effects=True, vmem_limit_bytes=62 * 1024 * 1024
        ),
    )(
        queries,
        flat_keys,
        flat_values,
        suffix_keys,
        suffix_values,
        suffix_lengths,
        slot_of_sample.reshape(1, samples),
        out_weight.T,
    )


def partial_softmax(scores, values_block, equation):
    row_max = jnp.max(scores, axis=-1)
    weights = jnp.exp(scores - row_max[..., None])
    row_total = jnp.sum(weights, axis=-1)
    output = jnp.einsum(
        equation, weights.astype(jnp.bfloat16), values_block, preferred_element_type=jnp.float32
    )
    return (output, row_max, row_total)


def per_device(
    queries,
    prompt_keys,
    prompt_values,
    suffix_keys,
    suffix_values,
    suffix_lengths,
    slot_of_sample,
    out_weight,
):
    local_count, heads_local, head_width = queries.shape
    kv_local = prompt_keys.shape[1]
    group_size = heads_local // kv_local
    score_scale = 1.0 / math.sqrt(head_width)
    all_queries = lax.all_gather(queries, "seq", axis=0, tiled=True)
    total_rows = all_queries.shape[0]
    block_rows = math.gcd(total_rows, 64)

    def prefix_block(query_block):
        grouped = query_block.reshape(block_rows, kv_local, group_size, head_width)
        scores = (
            jnp.einsum("bkgd,pkd->bkgp", grouped, prompt_keys, preferred_element_type=jnp.float32)
            * score_scale
        )
        output, row_max, row_total = partial_softmax(scores, prompt_values, "bkgp,pkd->bkgd")
        return (
            output.reshape(block_rows, heads_local, head_width),
            row_max.reshape(block_rows, heads_local),
            row_total.reshape(block_rows, heads_local),
        )

    blocks = all_queries.reshape(total_rows // block_rows, block_rows, heads_local, head_width)
    pre_out, pre_max, pre_total = lax.map(prefix_block, blocks)
    pre_out = pre_out.reshape(total_rows, heads_local, head_width)
    pre_max = pre_max.reshape(total_rows, heads_local)
    pre_total = pre_total.reshape(total_rows, heads_local)
    my_slots = lax.axis_index("seq") * local_count + jnp.arange(local_count, dtype=jnp.int32)
    matches = (slot_of_sample[None, :] == my_slots[:, None]).astype(jnp.int32)
    samples = jnp.sum(matches * jnp.arange(total_rows, dtype=jnp.int32)[None, :], axis=1)
    own_queries = all_queries[samples].reshape(local_count, kv_local, group_size, head_width)
    tail_scores = (
        jnp.einsum("bkgd,bksd->bkgs", own_queries, suffix_keys, preferred_element_type=jnp.float32)
        * score_scale
    )
    positions = jnp.arange(suffix_keys.shape[2], dtype=jnp.int32)
    live_mask = positions[None, None, None, :] < suffix_lengths[:, None, None, None]
    tail_scores = jnp.where(live_mask, tail_scores, jnp.float32(-1e30))
    tail_out, tail_max, tail_total = partial_softmax(tail_scores, suffix_values, "bkgs,bksd->bkgd")
    tail_out = tail_out.reshape(local_count, heads_local, head_width)
    tail_max = tail_max.reshape(local_count, heads_local)
    tail_total = tail_total.reshape(local_count, heads_local)
    old_max = pre_max[samples]
    joint_max = jnp.maximum(old_max, tail_max)
    old_factor = jnp.exp(old_max - joint_max)
    new_factor = jnp.exp(tail_max - joint_max)
    joint_out = pre_out[samples] * old_factor[..., None] + tail_out * new_factor[..., None]
    joint_total = pre_total[samples] * old_factor + tail_total * new_factor
    pre_out = pre_out.at[samples].set(joint_out)
    pre_max = pre_max.at[samples].set(joint_max)
    pre_total = pre_total.at[samples].set(joint_total)
    got_out, got_max, got_total = (
        lax.all_to_all(pre_out[None], "seq", split_axis=1, concat_axis=0, tiled=True),
        lax.all_to_all(pre_max[None], "seq", split_axis=1, concat_axis=0, tiled=True),
        lax.all_to_all(pre_total[None], "seq", split_axis=1, concat_axis=0, tiled=True),
    )
    best = jnp.max(got_max, axis=0)
    factors = jnp.exp(got_max - best[None])
    merged_out = jnp.sum(got_out * factors[..., None], axis=0)
    merged_total = jnp.sum(got_total * factors, axis=0)
    attention = (merged_out / merged_total[..., None]).astype(jnp.bfloat16)
    attention = attention.reshape(local_count, heads_local * head_width)
    terms = jnp.dot(
        lax.all_gather(attention, "seq", axis=0, tiled=True),
        out_weight,
        preferred_element_type=jnp.float32,
    )
    return lax.psum_scatter(terms, "head", scatter_dimension=0, tiled=True)


def solution(mesh):
    placed = (
        P("seq", "head", None),
        P("seq", "head", None),
        P("seq", "head", None),
        P("seq", "head", None, None),
        P("seq", "head", None, None),
        P("seq"),
        P(),
        P("head", "seq"),
    )

    def body(*arrays):
        kv = arrays[1].shape[1]
        fits = mesh.shape["seq"] == ZS * YS * CS and mesh.shape["head"] == 2 and kv == ZS
        return (fused if fits else per_device)(*arrays)

    return jax.shard_map(body, mesh=mesh, in_specs=placed, out_specs=P("head", "seq"), check_vma=False)
```

```python
import functools
import math

import jax
import jax.numpy as jnp
from jax import lax
from jax.experimental import pallas as pl
from jax.experimental.pallas import tpu as pltpu
from jax.sharding import PartitionSpec as P

MESH = pl.DeviceIdType.MESH
NT = (((1,), (1,)), ((), ()))
TN = (((0,), (0,)), ((), ()))
NN = (((1,), (0,)), ((), ()))
LOW = -1e30
ZS, YS, CS = 4, 2, 2


def dot(a, b, dims):
    return lax.dot_general(a, b, dims, preferred_element_type=jnp.float32)


def merge(parts, unit):
    top = functools.reduce(jnp.maximum, [part[1] for part in parts])
    out, total = None, None
    for part_out, part_top, part_total in parts:
        factor = jnp.exp2((part_top - top) * unit)
        scaled, count = part_out * factor, part_total * factor
        out = scaled if out is None else out + scaled
        total = count if total is None else total + count
    return out, top, total


def kernel(
    unit,
    q_in,
    keys_in,
    values_in,
    tail_keys_in,
    tail_values_in,
    lengths,
    slot_of,
    weight_in,
    out,
    q_own,
    raw_keys,
    raw_values,
    perm,
    match,
    q_all,
    keys,
    values,
    tail_keys,
    tail_values,
    weight,
    own_q,
    tail_scores,
    tail_rows,
    tail_out,
    tail_stat,
    part,
    stat,
    core_part,
    core_stat,
    y_own,
    y_send,
    y_part,
    y_own_stat,
    y_send_stat,
    y_stat,
    z_send,
    z_send_stat,
    z_part,
    z_stat,
    att,
    total,
    x_part,
    load_sem,
    tail_sem,
    q_sems,
    qz_send_sem,
    qz_recv_sem,
    core_sems,
    y_sems,
    zs_send,
    zs_recv,
    az_send,
    az_recv,
    a_sems,
    x_sems,
):
    kv_count, rows_local, width = q_own.shape
    slots = lengths.shape[0]
    group = rows_local // slots
    samples = slot_of.shape[1]
    chunk = YS * CS * rows_local
    lanes = part.shape[-1]
    thirds = chunk // lanes
    units = kv_count * thirds
    seq, head = lax.axis_index("seq"), lax.axis_index("head")
    z, y, core = seq // (YS * CS), (seq // CS) % YS, seq % CS
    other_y, other_core, other_head = 1 - y, 1 - core, 1 - head

    def at(z_to, y_to, core_to):
        return ((z_to * YS + y_to) * CS + core_to, head)

    z_peers = [at((z + step) % ZS, y, core) for step in range(1, ZS)]
    y_peer, core_peer, x_peer = at(z, other_y, core), at(z, y, other_core), (seq, other_head)
    order = [(3 * turn) % kv_count for turn in range(kv_count)]

    def remote(source, target, send, recv, device):
        return pltpu.make_async_remote_copy(
            src_ref=source, dst_ref=target, send_sem=send, recv_sem=recv, device_id=device, device_id_type=MESH
        )

    loads = [
        pltpu.make_async_copy(keys_in, raw_keys, load_sem.at[0]),
        pltpu.make_async_copy(values_in, raw_values, load_sem.at[1]),
        pltpu.make_async_copy(weight_in, weight, load_sem.at[2]),
    ]

    def tail_loads(k):
        return [
            pltpu.make_async_copy(tail_keys_in.at[:, k], tail_keys.at[k], tail_sem.at[k, 0]),
            pltpu.make_async_copy(tail_values_in.at[:, k], tail_values.at[k], tail_sem.at[k, 1]),
        ]

    loads[0].start()
    loads[1].start()
    for k in order:
        for load in tail_loads(k):
            load.start()
    loads[2].start()

    def grid(shape, axis):
        return lax.broadcasted_iota(jnp.int32, shape, axis)

    def onehot(chosen):
        return jnp.where(chosen, 1.0, 0.0).astype(jnp.bfloat16)

    flat = q_in[...].reshape(-1, width)
    shape = (rows_local, flat.shape[0])
    place = (grid(shape, 0) // group) * (kv_count * group) + grid(shape, 0) % group
    for k in order:
        q_own[k] = dot(onehot(grid(shape, 1) == place + k * group), flat, NN).astype(jnp.bfloat16)

    barrier = pltpu.get_barrier_semaphore()
    peers = z_peers + [y_peer, core_peer, x_peer]
    for peer in peers:
        pl.semaphore_signal(barrier, inc=1, device_id=peer, device_id_type=MESH)
    pl.semaphore_wait(barrier, len(peers))

    def block(y_of, core_of):
        return pl.ds((y_of * CS + core_of) * rows_local, rows_local)

    def q_z(k):
        return [
            remote(q_own.at[k], q_all.at[k, z, block(y, core)], qz_send_sem.at[k, i], qz_recv_sem.at[k, i], z_peers[i])
            for i in range(ZS - 1)
        ]

    def q_y(k):
        mine = q_all.at[k, :, block(y, core)]
        return remote(mine, mine, q_sems.at[k, 0], q_sems.at[k, 1], y_peer)

    def q_core(k):
        return [
            remote(
                q_all.at[k, :, block(i, core)],
                q_all.at[k, :, block(i, core)],
                q_sems.at[k, 2 + 2 * i],
                q_sems.at[k, 3 + 2 * i],
                core_peer,
            )
            for i in range(YS)
        ]

    for k in order:
        for copy in q_z(k):
            copy.start()
    for k in order:
        q_all[k, z, block(y, core), :] = q_own[k]

    def q_after_z(k):
        for copy in q_z(k):
            copy.wait()
        q_y(k).start()

    def q_after_y(k):
        q_y(k).wait()
        for copy in q_core(k):
            copy.start()

    def q_ready(k):
        for copy in q_core(k):
            copy.wait()

    def split_keys():
        size = 256 // kv_count
        shape = (256, 256)
        pick = onehot(grid(shape, 1) == (grid(shape, 0) % size) * kv_count + grid(shape, 0) // size)

        def one(i, carry):
            rows = raw_keys[pl.ds(pl.multiple_of(i * 256, 256), 256), :]
            apart = dot(pick, rows, NN).astype(jnp.bfloat16)
            for k in range(kv_count):
                keys[k, pl.ds(pl.multiple_of(i * size, size), size), :] = apart[k * size : (k + 1) * size]
            return carry

        lax.fori_loop(0, raw_keys.shape[0] // 256, one, 0, unroll=4)

    def split_values():
        wide = 128 * kv_count
        shape = (wide, wide)
        pick = onehot(grid(shape, 0) == (grid(shape, 1) % 128) * kv_count + grid(shape, 1) // 128)

        def one(i, carry):
            rows = raw_values[pl.ds(pl.multiple_of(i * wide, wide), wide), :]
            apart = dot(rows, pick, TN).astype(jnp.bfloat16)
            for k in range(kv_count):
                values[k, :width, pl.ds(pl.multiple_of(i * 128, 128), 128)] = apart[:, k * 128 : (k + 1) * 128]
            return carry

        lax.fori_loop(0, raw_values.shape[0] // wide, one, 0, unroll=2)
        for k in range(kv_count):
            values[k, width:, :] = jnp.ones((values.shape[1] - width, values.shape[2]), jnp.bfloat16)

    def prepare():
        columns = samples * group
        row_slot = seq * slots + grid((rows_local, samples), 0) // group
        shape = (samples, columns)
        spread = onehot(grid(shape, 1) // group == grid(shape, 0))
        wide = dot(onehot(slot_of[...] == row_slot), spread, NN)
        shape = (rows_local, columns)
        match[...] = jnp.where(grid(shape, 1) % group == grid(shape, 0) % group, wide, 0.0).astype(jnp.bfloat16)
        shape = (group, lanes // group, lanes)
        perm[...] = onehot(grid(shape, 2) == grid(shape, 1) * group + grid(shape, 0)).reshape(lanes, lanes)

    def tail(k):
        for load in tail_loads(k):
            load.wait()
        every = q_all[k].reshape(samples * group, width)
        own_q[...] = dot(match[...], every, NN)
        for t in range(slots):
            rows = slice(t * group, (t + 1) * group)
            scores = dot(own_q[rows, :].astype(jnp.bfloat16), tail_keys[k, t], NT)
            tail_scores[rows, :] = jnp.where(grid(scores.shape, 1) < lengths[t], scores, LOW)
        scores = tail_scores[...]
        top = jnp.max(scores, axis=1, keepdims=True)
        weights = jnp.exp2((scores - top) * unit)
        count = jnp.sum(weights, axis=1, keepdims=True)
        tail_scores[...] = weights
        for t in range(slots):
            rows = slice(t * group, (t + 1) * group)
            tail_rows[rows, :] = dot(tail_scores[rows, :].astype(jnp.bfloat16), tail_values[k, t], NN)
        for c in range(samples * group // chunk):
            place = match[:, c * chunk : (c + 1) * chunk]
            here = place.astype(jnp.float32) > 0.5
            rows = dot(tail_rows[...].astype(jnp.bfloat16), place, TN)
            best = jnp.max(jnp.where(here, top, LOW), axis=0, keepdims=True)
            sums = jnp.sum(jnp.where(here, count, 0.0), axis=0, keepdims=True)
            for r in range(thirds):
                span = slice(r * lanes, (r + 1) * lanes)
                tail_out[r, c] = rows[:, span]
                tail_stat[r, c, 0:1] = best[:, span]
                tail_stat[r, c, 1:2] = sums[:, span]

    def prompt(u, k, r):
        q = q_all[k, :, pl.ds(pl.multiple_of(r * lanes, lanes), lanes), :]
        pairs = ZS // 2
        scores = [dot(keys[k], q[2 * p : 2 * p + 2].reshape(2 * lanes, width), NT) for p in range(pairs)]
        for p in range(pairs):
            top = jnp.max(scores[p], axis=0, keepdims=True)
            weights = jnp.exp2((scores[p] - top) * unit).astype(jnp.bfloat16)
            both = dot(values[k], weights, NN)
            for c in range(2):
                span = slice(c * lanes, (c + 1) * lanes)
                at_chunk = p * 2 + c
                o, m, l = merge(
                    [
                        (both[:width, span], top[:, span], both[width : width + 1, span]),
                        (tail_out[r, at_chunk], tail_stat[r, at_chunk, 0:1], tail_stat[r, at_chunk, 1:2]),
                    ],
                    unit,
                )
                part[u, p, c] = o.astype(jnp.bfloat16)
                stat[u, p, c, 0:1] = m
                stat[u, p, c, 1:2] = l

    def sum_core(u):
        return [
            remote(part.at[u, :, other_core], core_part.at[u], core_sems.at[u, 0], core_sems.at[u, 1], core_peer),
            remote(stat.at[u, :, other_core], core_stat.at[u], core_sems.at[u, 2], core_sems.at[u, 3], core_peer),
        ]

    def sum_y(u):
        return [
            remote(y_send.at[u], y_part.at[u], y_sems.at[u, 0], y_sems.at[u, 1], y_peer),
            remote(y_send_stat.at[u], y_stat.at[u], y_sems.at[u, 2], y_sems.at[u, 3], y_peer),
        ]

    def head_of(u):
        return (3 * (u // thirds)) % kv_count

    def sum_z_out(u):
        k, r = head_of(u), u % thirds
        slot = (z - k + 2 * ZS - 1) % ZS
        return [
            remote(z_send.at[u], z_part.at[r, slot], zs_send.at[u, 0], zs_recv.at[r, slot, 0], at(k, y, core)),
            remote(z_send_stat.at[u], z_stat.at[r, slot], zs_send.at[u, 1], zs_recv.at[r, slot, 1], at(k, y, core)),
        ]

    def sum_z_in(u, slot):
        r = u % thirds
        return [
            remote(z_send.at[u], z_part.at[r, slot], zs_send.at[u, 0], zs_recv.at[r, slot, 0], y_peer),
            remote(z_send_stat.at[u], z_stat.at[r, slot], zs_send.at[u, 1], zs_recv.at[r, slot, 1], y_peer),
        ]

    def att_z(u, i):
        mine = att.at[u, y, core]
        return remote(mine, mine, az_send.at[u, i], az_recv.at[u], z_peers[i])

    def att_y(u):
        mine = att.at[u, y, core]
        return remote(mine, mine, a_sems.at[u, 0], a_sems.at[u, 1], y_peer)

    def att_core(u):
        mine = att.at[u, :, core]
        return remote(mine, mine, a_sems.at[u, 2], a_sems.at[u, 3], core_peer)

    def swap(r):
        rows = pl.ds(r * (lanes // group), lanes // group)
        return remote(
            total.at[pl.ds(2 * other_head, 2), rows],
            x_part.at[:, rows],
            x_sems.at[r, 0],
            x_sems.at[r, 1],
            x_peer,
        )

    def step_a(u):
        for copy in sum_core(u):
            copy.start()

    def step_b(u):
        for copy in sum_core(u):
            copy.wait()

        def joined(i):
            return merge(
                [
                    (part[u, i, core].astype(jnp.float32), stat[u, i, core, 0:1], stat[u, i, core, 1:2]),
                    (core_part[u, i].astype(jnp.float32), core_stat[u, i, 0:1], core_stat[u, i, 1:2]),
                ],
                unit,
            )

        o, m, l = joined(other_y)
        y_send[u] = o.astype(jnp.bfloat16)
        y_send_stat[u, 0:1] = m
        y_send_stat[u, 1:2] = l
        for copy in sum_y(u):
            copy.start()
        o, m, l = joined(y)
        y_own[u] = o
        y_own_stat[u, 0:1] = m
        y_own_stat[u, 1:2] = l

    def step_c(u):
        for copy in sum_y(u):
            copy.wait()
        o, m, l = merge(
            [
                (y_own[u], y_own_stat[u, 0:1], y_own_stat[u, 1:2]),
                (y_part[u].astype(jnp.float32), y_stat[u, 0:1], y_stat[u, 1:2]),
            ],
            unit,
        )
        y_own[u] = o
        z_send[u] = o.astype(jnp.bfloat16)
        z_send_stat[u, 0:1] = m
        z_send_stat[u, 1:2] = l

        @pl.when(z != head_of(u))
        def _():
            for copy in sum_z_out(u):
                copy.start()

    def step_d(u):
        @pl.when(z != head_of(u))
        def _():
            for copy in sum_z_out(u):
                copy.wait_send()

        @pl.when(z == head_of(u))
        def _():
            parts = [(y_own[u], z_send_stat[u, 0:1], z_send_stat[u, 1:2])]
            r = u % thirds
            for slot in range(ZS - 1):
                for copy in sum_z_in(u, slot):
                    copy.wait_recv()
                parts.append((z_part[r, slot].astype(jnp.float32), z_stat[r, slot, 0:1], z_stat[r, slot, 1:2]))
            o, _, l = merge(parts, unit)
            attention = (o / l).astype(jnp.bfloat16)
            rows = dot(perm[...], attention, NT).astype(jnp.bfloat16)
            att[u, y, core] = rows.reshape(att.shape[3:])
            for i in range(ZS - 1):
                att_z(u, i).start()

    def step_e(u):
        @pl.when(z != head_of(u))
        def _():
            att_z(u, 0).wait_recv()

        att_y(u).start()

    def step_f(u):
        @pl.when(z == head_of(u))
        def _():
            for i in range(ZS - 1):
                att_z(u, i).wait_send()

        att_y(u).wait()
        att_core(u).start()

    def step_g(u):
        att_core(u).wait()
        k, r = head_of(u), u % thirds
        value = None
        for g in range(0, group, 2):
            rows = jnp.concatenate(
                [
                    jnp.concatenate([att[u, i, j, g + h] for i in range(YS) for j in range(CS)], axis=0)
                    for h in range(2)
                ],
                axis=1,
            )
            first = pl.multiple_of((k * group + g) * width, 2 * width)
            term = dot(rows, weight[:, pl.ds(first, 2 * width)], NT)
            value = term if value is None else value + term
        count = lanes // group
        rows = pl.ds(pl.multiple_of(r * count, count), count)
        for c in range(ZS):
            total[c, rows, :] += value[c * count : (c + 1) * count]

        @pl.when(u >= units - thirds)
        def _():
            swap(r).start()

    a, b, c, d = order
    prepare()
    loads[0].wait()
    split_keys()
    q_after_z(a)
    loads[1].wait()
    split_values()
    q_after_y(a)
    q_after_z(b)
    q_ready(a)

    total[...] = jnp.zeros_like(total)
    loads[2].wait()
    q_hooks = {
        0: [(q_after_z, c), (q_after_y, b)],
        1: [(q_after_z, d)],
        2: [(q_ready, b), (q_after_y, c)],
        3: [(q_after_y, d)],
        5: [(q_ready, c)],
        8: [(q_ready, d)],
    }
    stages = [step_a, step_b, step_c, step_d, step_e, step_f, step_g]

    def turn(i, carry):
        @pl.when(i < units)
        def _():
            k, r = head_of(i), i % thirds

            @pl.when(r == 0)
            def _():
                tail(k)

            prompt(i, k, r)

        for late in reversed(range(len(stages))):

            @pl.when((i >= late) & (i < units + late))
            def _(late=late):
                stages[late](i - late)

        for at_turn, calls in q_hooks.items():

            @pl.when(i == at_turn)
            def _(calls=calls):
                for call, at_k in calls:
                    call(at_k)

        return carry

    lax.fori_loop(0, units + len(stages) - 1, turn, 0)
    for r in range(thirds):
        swap(r).wait()
    out[...] = (total[pl.ds(2 * head, 2)] + x_part[...]).reshape(out.shape)


def fused(queries, prompt_keys, prompt_values, suffix_keys, suffix_values, suffix_lengths, slot_of_sample, out_weight):
    slots, heads, width = queries.shape
    kv = prompt_keys.shape[1]
    group = heads // kv
    rows = slots * group
    positions = prompt_keys.shape[0]
    samples = slot_of_sample.shape[0]
    columns = samples * group
    chunk = YS * CS * rows
    lanes = 128
    thirds = chunk // lanes
    units = kv * thirds
    tail_len = suffix_keys.shape[2]
    half, out_columns = samples // 2, out_weight.shape[1]
    unit = math.log2(math.e) / math.sqrt(width)

    flat_keys = prompt_keys.reshape(positions * kv, width)
    flat_values = prompt_values.reshape(positions * kv, width)

    bf16, f32 = jnp.bfloat16, jnp.float32
    vmem, hbm = pl.BlockSpec(memory_space=pltpu.VMEM), pl.BlockSpec(memory_space=pl.ANY)
    sem = pltpu.SemaphoreType.DMA
    return pl.pallas_call(
        functools.partial(kernel, unit),
        out_shape=jax.ShapeDtypeStruct((half, out_columns), f32),
        in_specs=[vmem, hbm, hbm, hbm, hbm, pl.BlockSpec(memory_space=pltpu.SMEM), vmem, hbm],
        out_specs=vmem,
        scratch_shapes=[
            pltpu.VMEM((kv, rows, width), bf16),
            pltpu.VMEM(flat_keys.shape, bf16),
            pltpu.VMEM(flat_values.shape, bf16),
            pltpu.VMEM((lanes, lanes), bf16),
            pltpu.VMEM((rows, columns), bf16),
            pltpu.VMEM((kv, ZS, chunk, width), bf16),
            pltpu.VMEM((kv, positions, width), bf16),
            pltpu.VMEM((kv, width + 16, positions), bf16),
            pltpu.VMEM((kv, slots, tail_len, width), bf16),
            pltpu.VMEM((kv, slots, tail_len, width), bf16),
            pltpu.VMEM(out_weight.shape[::-1], bf16),
            pltpu.VMEM((rows, width), f32),
            pltpu.VMEM((rows, tail_len), f32),
            pltpu.VMEM((rows, width), f32),
            pltpu.VMEM((thirds, ZS, width, lanes), f32),
            pltpu.VMEM((thirds, ZS, 8, lanes), f32),
            pltpu.VMEM((units, YS, CS, width, lanes), bf16),
            pltpu.VMEM((units, YS, CS, 8, lanes), f32),
            pltpu.VMEM((units, YS, width, lanes), bf16),
            pltpu.VMEM((units, YS, 8, lanes), f32),
            pltpu.VMEM((units, width, lanes), f32),
            pltpu.VMEM((units, width, lanes), bf16),
            pltpu.VMEM((units, width, lanes), bf16),
            pltpu.VMEM((units, 8, lanes), f32),
            pltpu.VMEM((units, 8, lanes), f32),
            pltpu.VMEM((units, 8, lanes), f32),
            pltpu.VMEM((units, width, lanes), bf16),
            pltpu.VMEM((units, 8, lanes), f32),
            pltpu.VMEM((thirds, ZS - 1, width, lanes), bf16),
            pltpu.VMEM((thirds, ZS - 1, 8, lanes), f32),
            pltpu.VMEM((units, YS, CS, group, lanes // group, width), bf16),
            pltpu.VMEM((ZS, samples // ZS, out_columns), f32),
            pltpu.VMEM((2, samples // ZS, out_columns), f32),
            sem((3,)),
            sem((kv, 2)),
            sem((kv, 6)),
            sem((kv, ZS - 1)),
            sem((kv, ZS - 1)),
            sem((units, 4)),
            sem((units, 4)),
            sem((units, 2)),
            sem((thirds, ZS - 1, 2)),
            sem((units, ZS - 1)),
            sem((units,)),
            sem((units, 4)),
            sem((thirds, 2)),
        ],
        compiler_params=pltpu.CompilerParams(
            collective_id=0, has_side_effects=True, vmem_limit_bytes=62 * 1024 * 1024
        ),
    )(
        queries,
        flat_keys,
        flat_values,
        suffix_keys,
        suffix_values,
        suffix_lengths,
        slot_of_sample.reshape(1, samples),
        out_weight.T,
    )


def partial_softmax(scores, values_block, equation):
    row_max = jnp.max(scores, axis=-1)
    weights = jnp.exp(scores - row_max[..., None])
    row_total = jnp.sum(weights, axis=-1)
    output = jnp.einsum(
        equation, weights.astype(jnp.bfloat16), values_block, preferred_element_type=jnp.float32
    )
    return (output, row_max, row_total)


def per_device(
    queries,
    prompt_keys,
    prompt_values,
    suffix_keys,
    suffix_values,
    suffix_lengths,
    slot_of_sample,
    out_weight,
):
    local_count, heads_local, head_width = queries.shape
    kv_local = prompt_keys.shape[1]
    group_size = heads_local // kv_local
    score_scale = 1.0 / math.sqrt(head_width)
    all_queries = lax.all_gather(queries, "seq", axis=0, tiled=True)
    total_rows = all_queries.shape[0]
    block_rows = math.gcd(total_rows, 64)

    def prefix_block(query_block):
        grouped = query_block.reshape(block_rows, kv_local, group_size, head_width)
        scores = (
            jnp.einsum("bkgd,pkd->bkgp", grouped, prompt_keys, preferred_element_type=jnp.float32)
            * score_scale
        )
        output, row_max, row_total = partial_softmax(scores, prompt_values, "bkgp,pkd->bkgd")
        return (
            output.reshape(block_rows, heads_local, head_width),
            row_max.reshape(block_rows, heads_local),
            row_total.reshape(block_rows, heads_local),
        )

    blocks = all_queries.reshape(total_rows // block_rows, block_rows, heads_local, head_width)
    pre_out, pre_max, pre_total = lax.map(prefix_block, blocks)
    pre_out = pre_out.reshape(total_rows, heads_local, head_width)
    pre_max = pre_max.reshape(total_rows, heads_local)
    pre_total = pre_total.reshape(total_rows, heads_local)
    my_slots = lax.axis_index("seq") * local_count + jnp.arange(local_count, dtype=jnp.int32)
    matches = (slot_of_sample[None, :] == my_slots[:, None]).astype(jnp.int32)
    samples = jnp.sum(matches * jnp.arange(total_rows, dtype=jnp.int32)[None, :], axis=1)
    own_queries = all_queries[samples].reshape(local_count, kv_local, group_size, head_width)
    tail_scores = (
        jnp.einsum("bkgd,bksd->bkgs", own_queries, suffix_keys, preferred_element_type=jnp.float32)
        * score_scale
    )
    positions = jnp.arange(suffix_keys.shape[2], dtype=jnp.int32)
    live_mask = positions[None, None, None, :] < suffix_lengths[:, None, None, None]
    tail_scores = jnp.where(live_mask, tail_scores, jnp.float32(-1e30))
    tail_out, tail_max, tail_total = partial_softmax(tail_scores, suffix_values, "bkgs,bksd->bkgd")
    tail_out = tail_out.reshape(local_count, heads_local, head_width)
    tail_max = tail_max.reshape(local_count, heads_local)
    tail_total = tail_total.reshape(local_count, heads_local)
    old_max = pre_max[samples]
    joint_max = jnp.maximum(old_max, tail_max)
    old_factor = jnp.exp(old_max - joint_max)
    new_factor = jnp.exp(tail_max - joint_max)
    joint_out = pre_out[samples] * old_factor[..., None] + tail_out * new_factor[..., None]
    joint_total = pre_total[samples] * old_factor + tail_total * new_factor
    pre_out = pre_out.at[samples].set(joint_out)
    pre_max = pre_max.at[samples].set(joint_max)
    pre_total = pre_total.at[samples].set(joint_total)
    got_out, got_max, got_total = (
        lax.all_to_all(pre_out[None], "seq", split_axis=1, concat_axis=0, tiled=True),
        lax.all_to_all(pre_max[None], "seq", split_axis=1, concat_axis=0, tiled=True),
        lax.all_to_all(pre_total[None], "seq", split_axis=1, concat_axis=0, tiled=True),
    )
    best = jnp.max(got_max, axis=0)
    factors = jnp.exp(got_max - best[None])
    merged_out = jnp.sum(got_out * factors[..., None], axis=0)
    merged_total = jnp.sum(got_total * factors, axis=0)
    attention = (merged_out / merged_total[..., None]).astype(jnp.bfloat16)
    attention = attention.reshape(local_count, heads_local * head_width)
    terms = jnp.dot(
        lax.all_gather(attention, "seq", axis=0, tiled=True),
        out_weight,
        preferred_element_type=jnp.float32,
    )
    return lax.psum_scatter(terms, "head", scatter_dimension=0, tiled=True)


def solution(mesh):
    placed = (
        P("seq", "head", None),
        P("seq", "head", None),
        P("seq", "head", None),
        P("seq", "head", None, None),
        P("seq", "head", None, None),
        P("seq"),
        P(),
        P("head", "seq"),
    )

    def body(*arrays):
        kv = arrays[1].shape[1]
        fits = mesh.shape["seq"] == ZS * YS * CS and mesh.shape["head"] == 2 and kv == ZS
        return (fused if fits else per_device)(*arrays)

    return jax.shard_map(body, mesh=mesh, in_specs=placed, out_specs=P("head", "seq"), check_vma=False)
```

```python
import functools
import math

import jax
import jax.numpy as jnp
from jax import lax
from jax.experimental import pallas as pl
from jax.experimental.pallas import tpu as pltpu
from jax.sharding import PartitionSpec as P

MESH = pl.DeviceIdType.MESH
NT = (((1,), (1,)), ((), ()))
TN = (((0,), (0,)), ((), ()))
NN = (((1,), (0,)), ((), ()))
LOW = -1e30
ZS, YS, CS = 4, 2, 2


def dot(a, b, dims):
    return lax.dot_general(a, b, dims, preferred_element_type=jnp.float32)


def merge(parts, unit):
    top = functools.reduce(jnp.maximum, [part[1] for part in parts])
    out, total = None, None
    for part_out, part_top, part_total in parts:
        factor = jnp.exp2((part_top - top) * unit)
        scaled, count = part_out * factor, part_total * factor
        out = scaled if out is None else out + scaled
        total = count if total is None else total + count
    return out, top, total


def kernel(
    unit,
    q_in,
    keys_in,
    values_in,
    tail_keys_in,
    tail_values_in,
    lengths,
    slot_of,
    weight_in,
    out,
    q_own,
    raw_keys,
    raw_values,
    perm,
    match,
    q_all,
    keys,
    values,
    tail_keys,
    tail_values,
    weight,
    own_q,
    tail_scores,
    tail_rows,
    tail_out,
    tail_stat,
    scores_a,
    scores_b,
    weights_b,
    out_a,
    out_b,
    top_a,
    top_b,
    top_last,
    part,
    stat,
    core_part,
    core_stat,
    y_own,
    y_send,
    y_part,
    y_own_stat,
    y_send_stat,
    y_stat,
    z_send,
    z_send_stat,
    z_part,
    z_stat,
    att,
    total,
    x_part,
    load_sem,
    tail_sem,
    q_sems,
    qz_send_sem,
    qz_recv_sem,
    core_sems,
    y_sems,
    zs_send,
    zs_recv,
    az_send,
    az_recv,
    a_sems,
    x_sems,
):
    kv_count, rows_local, width = q_own.shape
    slots = lengths.shape[0]
    group = rows_local // slots
    samples = slot_of.shape[1]
    chunk = YS * CS * rows_local
    lanes = part.shape[-1]
    thirds = chunk // lanes
    units = kv_count * thirds
    seq, head = lax.axis_index("seq"), lax.axis_index("head")
    z, y, core = seq // (YS * CS), (seq // CS) % YS, seq % CS
    other_y, other_core, other_head = 1 - y, 1 - core, 1 - head

    def at(z_to, y_to, core_to):
        return ((z_to * YS + y_to) * CS + core_to, head)

    z_peers = [at((z + step) % ZS, y, core) for step in range(1, ZS)]
    y_peer, core_peer, x_peer = at(z, other_y, core), at(z, y, other_core), (seq, other_head)
    order = [(3 * turn) % kv_count for turn in range(kv_count)]

    def remote(source, target, send, recv, device):
        return pltpu.make_async_remote_copy(
            src_ref=source, dst_ref=target, send_sem=send, recv_sem=recv, device_id=device, device_id_type=MESH
        )

    loads = [
        pltpu.make_async_copy(keys_in, raw_keys, load_sem.at[0]),
        pltpu.make_async_copy(values_in, raw_values, load_sem.at[1]),
        pltpu.make_async_copy(weight_in, weight, load_sem.at[2]),
    ]

    def tail_loads(k):
        return [
            pltpu.make_async_copy(tail_keys_in.at[:, k], tail_keys.at[k], tail_sem.at[k, 0]),
            pltpu.make_async_copy(tail_values_in.at[:, k], tail_values.at[k], tail_sem.at[k, 1]),
        ]

    loads[0].start()
    loads[1].start()
    for k in order:
        for load in tail_loads(k):
            load.start()
    loads[2].start()

    def grid(shape, axis):
        return lax.broadcasted_iota(jnp.int32, shape, axis)

    def onehot(chosen):
        return jnp.where(chosen, 1.0, 0.0).astype(jnp.bfloat16)

    flat = q_in[...].reshape(-1, width)
    shape = (rows_local, flat.shape[0])
    place = (grid(shape, 0) // group) * (kv_count * group) + grid(shape, 0) % group
    for k in order:
        q_own[k] = dot(onehot(grid(shape, 1) == place + k * group), flat, NN).astype(jnp.bfloat16)

    barrier = pltpu.get_barrier_semaphore()
    peers = z_peers + [y_peer, core_peer, x_peer]
    for peer in peers:
        pl.semaphore_signal(barrier, inc=1, device_id=peer, device_id_type=MESH)
    pl.semaphore_wait(barrier, len(peers))

    def block(y_of, core_of):
        return pl.ds((y_of * CS + core_of) * rows_local, rows_local)

    def q_z(k):
        return [
            remote(q_own.at[k], q_all.at[k, z, block(y, core)], qz_send_sem.at[k, i], qz_recv_sem.at[k, i], z_peers[i])
            for i in range(ZS - 1)
        ]

    def q_y(k):
        mine = q_all.at[k, :, block(y, core)]
        return remote(mine, mine, q_sems.at[k, 0], q_sems.at[k, 1], y_peer)

    def q_core(k):
        return [
            remote(
                q_all.at[k, :, block(i, core)],
                q_all.at[k, :, block(i, core)],
                q_sems.at[k, 2 + 2 * i],
                q_sems.at[k, 3 + 2 * i],
                core_peer,
            )
            for i in range(YS)
        ]

    for copy in q_z(order[0]):
        copy.start()
    for k in order:
        q_all[k, z, block(y, core), :] = q_own[k]

    def q_start(k):
        for copy in q_z(k):
            copy.start()

    def q_after_z(k):
        for copy in q_z(k):
            copy.wait()
        q_y(k).start()

    def q_after_y(k):
        q_y(k).wait()
        for copy in q_core(k):
            copy.start()

    def q_ready(k):
        for copy in q_core(k):
            copy.wait()

    def split_keys():
        size = 256 // kv_count
        shape = (256, 256)
        pick = onehot(grid(shape, 1) == (grid(shape, 0) % size) * kv_count + grid(shape, 0) // size)

        def one(i, carry):
            rows = raw_keys[pl.ds(pl.multiple_of(i * 256, 256), 256), :]
            apart = dot(pick, rows, NN).astype(jnp.bfloat16)
            for k in range(kv_count):
                keys[k, pl.ds(pl.multiple_of(i * size, size), size), :] = apart[k * size : (k + 1) * size]
            return carry

        lax.fori_loop(0, raw_keys.shape[0] // 256, one, 0, unroll=4)

    def split_values():
        wide = 128 * kv_count
        shape = (wide, wide)
        pick = onehot(grid(shape, 0) == (grid(shape, 1) % 128) * kv_count + grid(shape, 1) // 128)

        def one(i, carry):
            rows = raw_values[pl.ds(pl.multiple_of(i * wide, wide), wide), :]
            apart = dot(rows, pick, TN).astype(jnp.bfloat16)
            for k in range(kv_count):
                values[k, :width, pl.ds(pl.multiple_of(i * 128, 128), 128)] = apart[:, k * 128 : (k + 1) * 128]
            return carry

        lax.fori_loop(0, raw_values.shape[0] // wide, one, 0, unroll=2)
        for k in range(kv_count):
            values[k, width:, :] = jnp.ones((values.shape[1] - width, values.shape[2]), jnp.bfloat16)

    def prepare():
        columns = samples * group
        row_slot = seq * slots + grid((rows_local, samples), 0) // group
        shape = (samples, columns)
        spread = onehot(grid(shape, 1) // group == grid(shape, 0))
        wide = dot(onehot(slot_of[...] == row_slot), spread, NN)
        shape = (rows_local, columns)
        match[...] = jnp.where(grid(shape, 1) % group == grid(shape, 0) % group, wide, 0.0).astype(jnp.bfloat16)
        shape = (group, lanes // group, lanes)
        perm[...] = onehot(grid(shape, 2) == grid(shape, 1) * group + grid(shape, 0)).reshape(lanes, lanes)

    def tail(k, base):
        for load in tail_loads(k):
            load.wait()
        every = q_all[k].reshape(samples * group, width)
        own_q[...] = dot(match[...], every, NN)
        for t in range(slots):
            rows = slice(t * group, (t + 1) * group)
            scores = dot(own_q[rows, :].astype(jnp.bfloat16), tail_keys[k, t], NT)
            tail_scores[rows, :] = jnp.where(grid(scores.shape, 1) < lengths[t], scores, LOW)
        scores = tail_scores[...]
        top = jnp.max(scores, axis=1, keepdims=True)
        weights = jnp.exp2((scores - top) * unit)
        count = jnp.sum(weights, axis=1, keepdims=True)
        tail_scores[...] = weights
        for t in range(slots):
            rows = slice(t * group, (t + 1) * group)
            tail_rows[rows, :] = dot(tail_scores[rows, :].astype(jnp.bfloat16), tail_values[k, t], NN)
        for c in range(samples * group // chunk):
            place = match[:, c * chunk : (c + 1) * chunk]
            here = place.astype(jnp.float32) > 0.5
            rows = dot(tail_rows[...].astype(jnp.bfloat16), place, TN)
            best = jnp.max(jnp.where(here, top, LOW), axis=0, keepdims=True)
            sums = jnp.sum(jnp.where(here, count, 0.0), axis=0, keepdims=True)
            for r in range(thirds):
                span = slice(r * lanes, (r + 1) * lanes)
                tail_out[base + r, c] = rows[:, span]
                tail_stat[base + r, c, 0:1] = best[:, span]
                tail_stat[base + r, c, 1:2] = sums[:, span]

    def scores_of(u, pair):
        k, r = head_of(u), u % thirds
        q = q_all[k, 2 * pair : 2 * pair + 2, pl.ds(pl.multiple_of(r * lanes, lanes), lanes), :]
        return dot(keys[k], q.reshape(2 * lanes, width), NT)

    def softmax(scores_ref, top_ref):
        scores = scores_ref[...]
        top = jnp.max(scores, axis=0, keepdims=True)
        top_ref[0:1] = top
        return jnp.exp2((scores - top) * unit).astype(jnp.bfloat16)

    def prompt(u):
        before, after = jnp.maximum(u - 1, 0), jnp.minimum(u + 1, units - 1)
        scores_b[...] = scores_of(u, 1)
        weights = softmax(scores_a, top_a)
        out_b[...] = dot(values[head_of(before)], weights_b[...], NN)
        top_last[...] = top_b[...]
        scores_a[...] = scores_of(after, 0)
        weights_b[...] = softmax(scores_b, top_b)
        out_a[...] = dot(values[head_of(u)], weights, NN)

    def prompt_last():
        out_b[...] = dot(values[head_of(units - 1)], weights_b[...], NN)
        top_last[...] = top_b[...]

    def store(u, pair, both, top, tails, tail_stats):
        for c in range(2):
            span = slice(c * lanes, (c + 1) * lanes)
            at_chunk = pair * 2 + c
            o, m, l = merge(
                [
                    (both[:width, span], top[0:1, span], both[width : width + 1, span]),
                    (tails[at_chunk], tail_stats[at_chunk, 0:1], tail_stats[at_chunk, 1:2]),
                ],
                unit,
            )
            part[u, pair, c] = o.astype(jnp.bfloat16)
            stat[u, pair, c, 0:1] = m
            stat[u, pair, c, 1:2] = l

    def sum_core(u):
        return [
            remote(part.at[u, :, other_core], core_part.at[u], core_sems.at[u, 0], core_sems.at[u, 1], core_peer),
            remote(stat.at[u, :, other_core], core_stat.at[u], core_sems.at[u, 2], core_sems.at[u, 3], core_peer),
        ]

    def sum_y(u):
        return [
            remote(y_send.at[u], y_part.at[u], y_sems.at[u, 0], y_sems.at[u, 1], y_peer),
            remote(y_send_stat.at[u], y_stat.at[u], y_sems.at[u, 2], y_sems.at[u, 3], y_peer),
        ]

    def head_of(u):
        return (3 * (u // thirds)) % kv_count

    def sum_z_out(u):
        k, r = head_of(u), u % thirds
        slot = (z - k + 2 * ZS - 1) % ZS
        return [
            remote(z_send.at[u], z_part.at[r, slot], zs_send.at[u, 0], zs_recv.at[r, slot, 0], at(k, y, core)),
            remote(z_send_stat.at[u], z_stat.at[r, slot], zs_send.at[u, 1], zs_recv.at[r, slot, 1], at(k, y, core)),
        ]

    def sum_z_in(u, slot):
        r = u % thirds
        return [
            remote(z_send.at[u], z_part.at[r, slot], zs_send.at[u, 0], zs_recv.at[r, slot, 0], y_peer),
            remote(z_send_stat.at[u], z_stat.at[r, slot], zs_send.at[u, 1], zs_recv.at[r, slot, 1], y_peer),
        ]

    def att_z(u, i):
        mine = att.at[u, y, core]
        return remote(mine, mine, az_send.at[u, i], az_recv.at[u], z_peers[i])

    def att_y(u):
        mine = att.at[u, y, core]
        return remote(mine, mine, a_sems.at[u, 0], a_sems.at[u, 1], y_peer)

    def att_core(u):
        mine = att.at[u, :, core]
        return remote(mine, mine, a_sems.at[u, 2], a_sems.at[u, 3], core_peer)

    def swap():
        return remote(total.at[pl.ds(2 * other_head, 2)], x_part, x_sems.at[0], x_sems.at[1], x_peer)

    def step_a(u):
        kept = ((u // thirds) % 2) * thirds + u % thirds
        store(u, 1, out_b, top_last, tail_out.at[kept], tail_stat.at[kept])
        for copy in sum_core(u):
            copy.start()

    def step_b(u):
        for copy in sum_core(u):
            copy.wait()

        def joined(i):
            return merge(
                [
                    (part[u, i, core].astype(jnp.float32), stat[u, i, core, 0:1], stat[u, i, core, 1:2]),
                    (core_part[u, i].astype(jnp.float32), core_stat[u, i, 0:1], core_stat[u, i, 1:2]),
                ],
                unit,
            )

        o, m, l = joined(other_y)
        y_send[u] = o.astype(jnp.bfloat16)
        y_send_stat[u, 0:1] = m
        y_send_stat[u, 1:2] = l
        for copy in sum_y(u):
            copy.start()
        o, m, l = joined(y)
        y_own[u] = o
        y_own_stat[u, 0:1] = m
        y_own_stat[u, 1:2] = l

    def step_c(u):
        for copy in sum_y(u):
            copy.wait()
        o, m, l = merge(
            [
                (y_own[u], y_own_stat[u, 0:1], y_own_stat[u, 1:2]),
                (y_part[u].astype(jnp.float32), y_stat[u, 0:1], y_stat[u, 1:2]),
            ],
            unit,
        )
        y_own[u] = o
        z_send[u] = o.astype(jnp.bfloat16)
        z_send_stat[u, 0:1] = m
        z_send_stat[u, 1:2] = l

        @pl.when(z != head_of(u))
        def _():
            for copy in sum_z_out(u):
                copy.start()

    def step_d(u):
        @pl.when(z != head_of(u))
        def _():
            for copy in sum_z_out(u):
                copy.wait_send()

        @pl.when(z == head_of(u))
        def _():
            parts = [(y_own[u], z_send_stat[u, 0:1], z_send_stat[u, 1:2])]
            r = u % thirds
            for slot in range(ZS - 1):
                for copy in sum_z_in(u, slot):
                    copy.wait_recv()
                parts.append((z_part[r, slot].astype(jnp.float32), z_stat[r, slot, 0:1], z_stat[r, slot, 1:2]))
            o, _, l = merge(parts, unit)
            attention = (o / l).astype(jnp.bfloat16)
            rows = dot(perm[...], attention, NT).astype(jnp.bfloat16)
            att[u, y, core] = rows.reshape(att.shape[3:])
            for i in range(ZS - 1):
                att_z(u, i).start()

    def step_e(u):
        @pl.when(z != head_of(u))
        def _():
            att_z(u, 0).wait_recv()

        att_y(u).start()

    def step_f(u):
        @pl.when(z == head_of(u))
        def _():
            for i in range(ZS - 1):
                att_z(u, i).wait_send()

        att_y(u).wait()
        att_core(u).start()

    def step_g(u):
        att_core(u).wait()

        @pl.when(u % thirds == thirds - 1)
        def _():
            project(u // thirds)

    def project(turn_of):
        k = (3 * turn_of) % kv_count
        value = None
        for g in range(0, group, 2):
            rows = jnp.concatenate(
                [
                    jnp.concatenate(
                        [
                            att[turn_of * thirds + r, i, j, g + h]
                            for i in range(YS)
                            for j in range(CS)
                            for r in range(thirds)
                        ],
                        axis=0,
                    )
                    for h in range(2)
                ],
                axis=1,
            )
            first = pl.multiple_of((k * group + g) * width, 2 * width)
            term = dot(rows, weight[:, pl.ds(first, 2 * width)], NT)
            value = term if value is None else value + term
        total[...] += value.reshape(total.shape)

    a, b, c, d = order
    prepare()
    loads[0].wait()
    split_keys()
    q_after_z(a)
    q_start(b)
    loads[1].wait()
    split_values()
    q_after_y(a)
    q_start(c)
    q_start(d)
    q_ready(a)
    scores_a[...] = scores_of(0, 0)

    total[...] = jnp.zeros_like(total)
    loads[2].wait()
    q_hooks = {
        0: [(q_after_z, b), (q_after_z, c)],
        1: [(q_after_y, b), (q_ready, b), (q_after_z, d)],
        2: [(q_after_y, c)],
        3: [(q_after_y, d)],
        4: [(q_ready, c)],
        7: [(q_ready, d)],
    }
    stages = [step_a, step_b, step_c, step_d, step_e, step_f, step_g]

    def turn(i, carry):
        @pl.when(i < units)
        def _():
            k, r = head_of(i), i % thirds

            @pl.when(r == 0)
            def _():
                tail(k, ((i // thirds) % 2) * thirds)

            prompt(i)
            kept = ((i // thirds) % 2) * thirds + r
            store(i, 0, out_a, top_a, tail_out.at[kept], tail_stat.at[kept])

        @pl.when(i == units)
        def _():
            prompt_last()

        for late in reversed(range(len(stages))):

            @pl.when((i > late) & (i <= units + late))
            def _(late=late):
                stages[late](i - late - 1)

        for at_turn, calls in q_hooks.items():

            @pl.when(i == at_turn)
            def _(calls=calls):
                for call, at_k in calls:
                    call(at_k)

        return carry

    lax.fori_loop(0, units + len(stages), turn, 0)
    swap().start()
    swap().wait()
    out[...] = (total[pl.ds(2 * head, 2)] + x_part[...]).reshape(out.shape)


def fused(queries, prompt_keys, prompt_values, suffix_keys, suffix_values, suffix_lengths, slot_of_sample, out_weight):
    slots, heads, width = queries.shape
    kv = prompt_keys.shape[1]
    group = heads // kv
    rows = slots * group
    positions = prompt_keys.shape[0]
    samples = slot_of_sample.shape[0]
    columns = samples * group
    chunk = YS * CS * rows
    lanes = 128
    thirds = chunk // lanes
    units = kv * thirds
    tail_len = suffix_keys.shape[2]
    half, out_columns = samples // 2, out_weight.shape[1]
    unit = math.log2(math.e) / math.sqrt(width)

    flat_keys = prompt_keys.reshape(positions * kv, width)
    flat_values = prompt_values.reshape(positions * kv, width)

    bf16, f32 = jnp.bfloat16, jnp.float32
    vmem, hbm = pl.BlockSpec(memory_space=pltpu.VMEM), pl.BlockSpec(memory_space=pl.ANY)
    sem = pltpu.SemaphoreType.DMA
    return pl.pallas_call(
        functools.partial(kernel, unit),
        out_shape=jax.ShapeDtypeStruct((half, out_columns), f32),
        in_specs=[vmem, hbm, hbm, hbm, hbm, pl.BlockSpec(memory_space=pltpu.SMEM), vmem, hbm],
        out_specs=vmem,
        scratch_shapes=[
            pltpu.VMEM((kv, rows, width), bf16),
            pltpu.VMEM(flat_keys.shape, bf16),
            pltpu.VMEM(flat_values.shape, bf16),
            pltpu.VMEM((lanes, lanes), bf16),
            pltpu.VMEM((rows, columns), bf16),
            pltpu.VMEM((kv, ZS, chunk, width), bf16),
            pltpu.VMEM((kv, positions, width), bf16),
            pltpu.VMEM((kv, width + 16, positions), bf16),
            pltpu.VMEM((kv, slots, tail_len, width), bf16),
            pltpu.VMEM((kv, slots, tail_len, width), bf16),
            pltpu.VMEM(out_weight.shape[::-1], bf16),
            pltpu.VMEM((rows, width), f32),
            pltpu.VMEM((rows, tail_len), f32),
            pltpu.VMEM((rows, width), f32),
            pltpu.VMEM((2 * thirds, ZS, width, lanes), f32),
            pltpu.VMEM((2 * thirds, ZS, 8, lanes), f32),
            pltpu.VMEM((positions, 2 * lanes), f32),
            pltpu.VMEM((positions, 2 * lanes), f32),
            pltpu.VMEM((positions, 2 * lanes), bf16),
            pltpu.VMEM((width + 16, 2 * lanes), f32),
            pltpu.VMEM((width + 16, 2 * lanes), f32),
            pltpu.VMEM((8, 2 * lanes), f32),
            pltpu.VMEM((8, 2 * lanes), f32),
            pltpu.VMEM((8, 2 * lanes), f32),
            pltpu.VMEM((units, YS, CS, width, lanes), bf16),
            pltpu.VMEM((units, YS, CS, 8, lanes), f32),
            pltpu.VMEM((units, YS, width, lanes), bf16),
            pltpu.VMEM((units, YS, 8, lanes), f32),
            pltpu.VMEM((units, width, lanes), f32),
            pltpu.VMEM((units, width, lanes), bf16),
            pltpu.VMEM((units, width, lanes), bf16),
            pltpu.VMEM((units, 8, lanes), f32),
            pltpu.VMEM((units, 8, lanes), f32),
            pltpu.VMEM((units, 8, lanes), f32),
            pltpu.VMEM((units, width, lanes), bf16),
            pltpu.VMEM((units, 8, lanes), f32),
            pltpu.VMEM((thirds, ZS - 1, width, lanes), bf16),
            pltpu.VMEM((thirds, ZS - 1, 8, lanes), f32),
            pltpu.VMEM((units, YS, CS, group, lanes // group, width), bf16),
            pltpu.VMEM((ZS, samples // ZS, out_columns), f32),
            pltpu.VMEM((2, samples // ZS, out_columns), f32),
            sem((3,)),
            sem((kv, 2)),
            sem((kv, 6)),
            sem((kv, ZS - 1)),
            sem((kv, ZS - 1)),
            sem((units, 4)),
            sem((units, 4)),
            sem((units, 2)),
            sem((thirds, ZS - 1, 2)),
            sem((units, ZS - 1)),
            sem((units,)),
            sem((units, 4)),
            sem((2,)),
        ],
        compiler_params=pltpu.CompilerParams(
            collective_id=0, has_side_effects=True, vmem_limit_bytes=62 * 1024 * 1024
        ),
    )(
        queries,
        flat_keys,
        flat_values,
        suffix_keys,
        suffix_values,
        suffix_lengths,
        slot_of_sample.reshape(1, samples),
        out_weight.T,
    )


def partial_softmax(scores, values_block, equation):
    row_max = jnp.max(scores, axis=-1)
    weights = jnp.exp(scores - row_max[..., None])
    row_total = jnp.sum(weights, axis=-1)
    output = jnp.einsum(
        equation, weights.astype(jnp.bfloat16), values_block, preferred_element_type=jnp.float32
    )
    return (output, row_max, row_total)


def per_device(
    queries,
    prompt_keys,
    prompt_values,
    suffix_keys,
    suffix_values,
    suffix_lengths,
    slot_of_sample,
    out_weight,
):
    local_count, heads_local, head_width = queries.shape
    kv_local = prompt_keys.shape[1]
    group_size = heads_local // kv_local
    score_scale = 1.0 / math.sqrt(head_width)
    all_queries = lax.all_gather(queries, "seq", axis=0, tiled=True)
    total_rows = all_queries.shape[0]
    block_rows = math.gcd(total_rows, 64)

    def prefix_block(query_block):
        grouped = query_block.reshape(block_rows, kv_local, group_size, head_width)
        scores = (
            jnp.einsum("bkgd,pkd->bkgp", grouped, prompt_keys, preferred_element_type=jnp.float32)
            * score_scale
        )
        output, row_max, row_total = partial_softmax(scores, prompt_values, "bkgp,pkd->bkgd")
        return (
            output.reshape(block_rows, heads_local, head_width),
            row_max.reshape(block_rows, heads_local),
            row_total.reshape(block_rows, heads_local),
        )

    blocks = all_queries.reshape(total_rows // block_rows, block_rows, heads_local, head_width)
    pre_out, pre_max, pre_total = lax.map(prefix_block, blocks)
    pre_out = pre_out.reshape(total_rows, heads_local, head_width)
    pre_max = pre_max.reshape(total_rows, heads_local)
    pre_total = pre_total.reshape(total_rows, heads_local)
    my_slots = lax.axis_index("seq") * local_count + jnp.arange(local_count, dtype=jnp.int32)
    matches = (slot_of_sample[None, :] == my_slots[:, None]).astype(jnp.int32)
    samples = jnp.sum(matches * jnp.arange(total_rows, dtype=jnp.int32)[None, :], axis=1)
    own_queries = all_queries[samples].reshape(local_count, kv_local, group_size, head_width)
    tail_scores = (
        jnp.einsum("bkgd,bksd->bkgs", own_queries, suffix_keys, preferred_element_type=jnp.float32)
        * score_scale
    )
    positions = jnp.arange(suffix_keys.shape[2], dtype=jnp.int32)
    live_mask = positions[None, None, None, :] < suffix_lengths[:, None, None, None]
    tail_scores = jnp.where(live_mask, tail_scores, jnp.float32(-1e30))
    tail_out, tail_max, tail_total = partial_softmax(tail_scores, suffix_values, "bkgs,bksd->bkgd")
    tail_out = tail_out.reshape(local_count, heads_local, head_width)
    tail_max = tail_max.reshape(local_count, heads_local)
    tail_total = tail_total.reshape(local_count, heads_local)
    old_max = pre_max[samples]
    joint_max = jnp.maximum(old_max, tail_max)
    old_factor = jnp.exp(old_max - joint_max)
    new_factor = jnp.exp(tail_max - joint_max)
    joint_out = pre_out[samples] * old_factor[..., None] + tail_out * new_factor[..., None]
    joint_total = pre_total[samples] * old_factor + tail_total * new_factor
    pre_out = pre_out.at[samples].set(joint_out)
    pre_max = pre_max.at[samples].set(joint_max)
    pre_total = pre_total.at[samples].set(joint_total)
    got_out, got_max, got_total = (
        lax.all_to_all(pre_out[None], "seq", split_axis=1, concat_axis=0, tiled=True),
        lax.all_to_all(pre_max[None], "seq", split_axis=1, concat_axis=0, tiled=True),
        lax.all_to_all(pre_total[None], "seq", split_axis=1, concat_axis=0, tiled=True),
    )
    best = jnp.max(got_max, axis=0)
    factors = jnp.exp(got_max - best[None])
    merged_out = jnp.sum(got_out * factors[..., None], axis=0)
    merged_total = jnp.sum(got_total * factors, axis=0)
    attention = (merged_out / merged_total[..., None]).astype(jnp.bfloat16)
    attention = attention.reshape(local_count, heads_local * head_width)
    terms = jnp.dot(
        lax.all_gather(attention, "seq", axis=0, tiled=True),
        out_weight,
        preferred_element_type=jnp.float32,
    )
    return lax.psum_scatter(terms, "head", scatter_dimension=0, tiled=True)


def solution(mesh):
    placed = (
        P("seq", "head", None),
        P("seq", "head", None),
        P("seq", "head", None),
        P("seq", "head", None, None),
        P("seq", "head", None, None),
        P("seq"),
        P(),
        P("head", "seq"),
    )

    def body(*arrays):
        kv = arrays[1].shape[1]
        fits = mesh.shape["seq"] == ZS * YS * CS and mesh.shape["head"] == 2 and kv == ZS
        return (fused if fits else per_device)(*arrays)

    return jax.shard_map(body, mesh=mesh, in_specs=placed, out_specs=P("head", "seq"), check_vma=False)
```

```python
import functools
import math

import jax
import jax.numpy as jnp
from jax import lax
from jax.experimental import pallas as pl
from jax.experimental.pallas import tpu as pltpu
from jax.sharding import PartitionSpec as P

MESH = pl.DeviceIdType.MESH
NT = (((1,), (1,)), ((), ()))
TN = (((0,), (0,)), ((), ()))
NN = (((1,), (0,)), ((), ()))
LOW = -1e30
ZS, YS, CS = 4, 2, 2


def dot(a, b, dims):
    return lax.dot_general(a, b, dims, preferred_element_type=jnp.float32)


def merge(parts, unit):
    top = functools.reduce(jnp.maximum, [part[1] for part in parts])
    out, total = None, None
    for part_out, part_top, part_total in parts:
        factor = jnp.exp2((part_top - top) * unit)
        scaled, count = part_out * factor, part_total * factor
        out = scaled if out is None else out + scaled
        total = count if total is None else total + count
    return out, top, total


def kernel(
    unit,
    q_in,
    keys_in,
    values_in,
    tail_keys_in,
    tail_values_in,
    lengths,
    slot_of,
    weight_in,
    out,
    q_own,
    raw_keys,
    raw_values,
    perm,
    match,
    q_all,
    keys,
    values,
    tail_keys,
    tail_values,
    weight,
    own_q,
    tail_scores,
    tail_rows,
    tail_out,
    tail_stat,
    part,
    stat,
    near_part,
    near_stat,
    z_own,
    z_send,
    z_send_stat,
    z_part,
    z_stat,
    att,
    total,
    x_part,
    load_sem,
    tail_sem,
    qz_sems,
    qn_sems,
    near_sems,
    z_sems,
    att_sems,
    x_sems,
):
    kv_count, rows_local, width = q_own.shape
    slots = lengths.shape[0]
    group = rows_local // slots
    samples = slot_of.shape[1]
    chunk = YS * CS * rows_local
    lanes = part.shape[-1]
    thirds = chunk // lanes
    units = kv_count * thirds
    seq, head = lax.axis_index("seq"), lax.axis_index("head")
    z, y, core = seq // (YS * CS), (seq // CS) % YS, seq % CS
    other_head = 1 - head

    def at(z_to, y_to, core_to):
        return ((z_to * YS + y_to) * CS + core_to, head)

    z_peers = [at((z + step) % ZS, y, core) for step in range(1, ZS)]
    near = [((y + step // CS) % YS, (core + step % CS) % CS) for step in range(1, YS * CS)]
    near_peers = [at(z, *place) for place in near]
    x_peer = (seq, other_head)
    order = [(3 * turn) % kv_count for turn in range(kv_count)]

    def remote(source, target, send, recv, device):
        return pltpu.make_async_remote_copy(
            src_ref=source, dst_ref=target, send_sem=send, recv_sem=recv, device_id=device, device_id_type=MESH
        )

    loads = [
        pltpu.make_async_copy(keys_in, raw_keys, load_sem.at[0]),
        pltpu.make_async_copy(values_in, raw_values, load_sem.at[1]),
        pltpu.make_async_copy(weight_in, weight, load_sem.at[2]),
    ]

    def tail_loads(k):
        return [
            pltpu.make_async_copy(tail_keys_in.at[:, k], tail_keys.at[k], tail_sem.at[k, 0]),
            pltpu.make_async_copy(tail_values_in.at[:, k], tail_values.at[k], tail_sem.at[k, 1]),
        ]

    loads[0].start()
    loads[1].start()
    for k in order:
        for load in tail_loads(k):
            load.start()
    loads[2].start()

    def grid(shape, axis):
        return lax.broadcasted_iota(jnp.int32, shape, axis)

    def onehot(chosen):
        return jnp.where(chosen, 1.0, 0.0).astype(jnp.bfloat16)

    flat = q_in[...].reshape(-1, width)
    shape = (rows_local, flat.shape[0])
    place = (grid(shape, 0) // group) * (kv_count * group) + grid(shape, 0) % group
    for k in order:
        q_own[k] = dot(onehot(grid(shape, 1) == place + k * group), flat, NN).astype(jnp.bfloat16)

    barrier = pltpu.get_barrier_semaphore()
    peers = z_peers + near_peers + [x_peer]
    for peer in peers:
        pl.semaphore_signal(barrier, inc=1, device_id=peer, device_id_type=MESH)
    pl.semaphore_wait(barrier, len(peers))

    def block(y_of, core_of):
        return pl.ds((y_of * CS + core_of) * rows_local, rows_local)

    def q_z(k):
        return [
            remote(
                q_own.at[k], q_all.at[k, z, block(y, core)], qz_sems.at[k, i, 0], qz_sems.at[k, i, 1], z_peers[i]
            )
            for i in range(ZS - 1)
        ]

    def q_near(k):
        mine = q_all.at[k, :, block(y, core)]
        return [
            remote(mine, mine, qn_sems.at[k, i, 0], qn_sems.at[k, i, 1], near_peers[i]) for i in range(YS * CS - 1)
        ]

    def start(copies):
        for copy in copies:
            copy.start()

    def wait(copies):
        for copy in copies:
            copy.wait()

    start(q_z(order[0]))
    for k in order:
        q_all[k, z, block(y, core), :] = q_own[k]

    def q_after_z(k):
        wait(q_z(k))
        start(q_near(k))

    def q_ready(k):
        wait(q_near(k))

    def split_keys():
        size = 256 // kv_count
        shape = (256, 256)
        pick = onehot(grid(shape, 1) == (grid(shape, 0) % size) * kv_count + grid(shape, 0) // size)

        def one(i, carry):
            rows = raw_keys[pl.ds(pl.multiple_of(i * 256, 256), 256), :]
            apart = dot(pick, rows, NN).astype(jnp.bfloat16)
            for k in range(kv_count):
                keys[k, pl.ds(pl.multiple_of(i * size, size), size), :] = apart[k * size : (k + 1) * size]
            return carry

        lax.fori_loop(0, raw_keys.shape[0] // 256, one, 0, unroll=4)

    def split_values():
        wide = 128 * kv_count
        shape = (wide, wide)
        pick = onehot(grid(shape, 0) == (grid(shape, 1) % 128) * kv_count + grid(shape, 1) // 128)

        def one(i, carry):
            rows = raw_values[pl.ds(pl.multiple_of(i * wide, wide), wide), :]
            apart = dot(rows, pick, TN).astype(jnp.bfloat16)
            for k in range(kv_count):
                values[k, :width, pl.ds(pl.multiple_of(i * 128, 128), 128)] = apart[:, k * 128 : (k + 1) * 128]
            return carry

        lax.fori_loop(0, raw_values.shape[0] // wide, one, 0, unroll=2)
        for k in range(kv_count):
            values[k, width:, :] = jnp.ones((values.shape[1] - width, values.shape[2]), jnp.bfloat16)

    def prepare():
        columns = samples * group
        row_slot = seq * slots + grid((rows_local, samples), 0) // group
        shape = (samples, columns)
        spread = onehot(grid(shape, 1) // group == grid(shape, 0))
        wide = dot(onehot(slot_of[...] == row_slot), spread, NN)
        shape = (rows_local, columns)
        match[...] = jnp.where(grid(shape, 1) % group == grid(shape, 0) % group, wide, 0.0).astype(jnp.bfloat16)
        shape = (group, lanes // group, lanes)
        perm[...] = onehot(grid(shape, 2) == grid(shape, 1) * group + grid(shape, 0)).reshape(lanes, lanes)

    def tail(k):
        for load in tail_loads(k):
            load.wait()
        every = q_all[k].reshape(samples * group, width)
        own_q[...] = dot(match[...], every, NN)
        for t in range(slots):
            rows = slice(t * group, (t + 1) * group)
            scores = dot(own_q[rows, :].astype(jnp.bfloat16), tail_keys[k, t], NT)
            tail_scores[rows, :] = jnp.where(grid(scores.shape, 1) < lengths[t], scores, LOW)
        scores = tail_scores[...]
        top = jnp.max(scores, axis=1, keepdims=True)
        weights = jnp.exp2((scores - top) * unit)
        count = jnp.sum(weights, axis=1, keepdims=True)
        tail_scores[...] = weights
        for t in range(slots):
            rows = slice(t * group, (t + 1) * group)
            tail_rows[rows, :] = dot(tail_scores[rows, :].astype(jnp.bfloat16), tail_values[k, t], NN)
        for c in range(samples * group // chunk):
            place = match[:, c * chunk : (c + 1) * chunk]
            here = place.astype(jnp.float32) > 0.5
            rows = dot(tail_rows[...].astype(jnp.bfloat16), place, TN)
            best = jnp.max(jnp.where(here, top, LOW), axis=0, keepdims=True)
            sums = jnp.sum(jnp.where(here, count, 0.0), axis=0, keepdims=True)
            for r in range(thirds):
                span = slice(r * lanes, (r + 1) * lanes)
                tail_out[r, c] = rows[:, span]
                tail_stat[r, c, 0:1] = best[:, span]
                tail_stat[r, c, 1:2] = sums[:, span]

    def prompt(u, k, r):
        q = q_all[k, :, pl.ds(pl.multiple_of(r * lanes, lanes), lanes), :]
        pairs = ZS // 2
        scores = [dot(keys[k], q[2 * p : 2 * p + 2].reshape(2 * lanes, width), NT) for p in range(pairs)]
        for p in range(pairs):
            top = jnp.max(scores[p], axis=0, keepdims=True)
            weights = jnp.exp2((scores[p] - top) * unit).astype(jnp.bfloat16)
            both = dot(values[k], weights, NN)
            for c in range(2):
                span = slice(c * lanes, (c + 1) * lanes)
                at_chunk = p * 2 + c
                o, m, l = merge(
                    [
                        (both[:width, span], top[:, span], both[width : width + 1, span]),
                        (tail_out[r, at_chunk], tail_stat[r, at_chunk, 0:1], tail_stat[r, at_chunk, 1:2]),
                    ],
                    unit,
                )
                part[u, p, c] = o.astype(jnp.bfloat16)
                stat[u, p, c, 0:1] = m
                stat[u, p, c, 1:2] = l

    def head_of(u):
        return (3 * (u // thirds)) % kv_count

    def sum_near(u):
        copies = []
        for i, (y_to, core_to) in enumerate(near):
            sems = near_sems.at[u, i]
            copies += [
                remote(part.at[u, y_to, core_to], near_part.at[u, i], sems.at[0], sems.at[1], near_peers[i]),
                remote(stat.at[u, y_to, core_to], near_stat.at[u, i], sems.at[2], sems.at[3], near_peers[i]),
            ]
        return copies

    def sum_z(u):
        copies = []
        for i in range(ZS - 1):
            sems = z_sems.at[u, i]
            copies += [
                remote(z_send.at[u], z_part.at[u, i], sems.at[0], sems.at[1], z_peers[i]),
                remote(z_send_stat.at[u], z_stat.at[u, i], sems.at[2], sems.at[3], z_peers[i]),
            ]
        return copies

    def att_near(u):
        mine = att.at[u, y, core]
        return [
            remote(mine, mine, att_sems.at[u, i, 0], att_sems.at[u, i, 1], near_peers[i]) for i in range(YS * CS - 1)
        ]

    def swap():
        return remote(total.at[pl.ds(2 * other_head, 2)], x_part, x_sems.at[0], x_sems.at[1], x_peer)

    def step_a(u):
        start(sum_near(u))

    def step_b(u):
        wait(sum_near(u))
        parts = [(part[u, y, core].astype(jnp.float32), stat[u, y, core, 0:1], stat[u, y, core, 1:2])]
        for i in range(YS * CS - 1):
            parts.append((near_part[u, i].astype(jnp.float32), near_stat[u, i, 0:1], near_stat[u, i, 1:2]))
        o, m, l = merge(parts, unit)
        z_own[u] = o
        z_send[u] = o.astype(jnp.bfloat16)
        z_send_stat[u, 0:1] = m
        z_send_stat[u, 1:2] = l
        start(sum_z(u))

    def step_c(u):
        wait(sum_z(u))
        parts = [(z_own[u], z_send_stat[u, 0:1], z_send_stat[u, 1:2])]
        for i in range(ZS - 1):
            parts.append((z_part[u, i].astype(jnp.float32), z_stat[u, i, 0:1], z_stat[u, i, 1:2]))
        o, _, l = merge(parts, unit)
        attention = (o / l).astype(jnp.bfloat16)
        rows = dot(perm[...], attention, NT).astype(jnp.bfloat16)
        att[u, y, core] = rows.reshape(att.shape[3:])
        start(att_near(u))

    def step_d(u):
        wait(att_near(u))

        @pl.when(u % thirds == thirds - 1)
        def _():
            project(u // thirds)

    def project(turn_of):
        k = (3 * turn_of) % kv_count
        value = None
        for g in range(0, group, 2):
            rows = jnp.concatenate(
                [
                    jnp.concatenate(
                        [
                            att[turn_of * thirds + r, i, j, g + h]
                            for i in range(YS)
                            for j in range(CS)
                            for r in range(thirds)
                        ],
                        axis=0,
                    )
                    for h in range(2)
                ],
                axis=1,
            )
            first = pl.multiple_of((k * group + g) * width, 2 * width)
            term = dot(rows, weight[:, pl.ds(first, 2 * width)], NT)
            value = term if value is None else value + term
        total[...] += value.reshape(total.shape)

    a, b, c, d = order
    prepare()
    for k in order[1:]:
        start(q_z(k))
    loads[0].wait()
    split_keys()
    q_after_z(a)
    loads[1].wait()
    split_values()
    q_after_z(b)
    q_ready(a)
    total[...] = jnp.zeros_like(total)
    loads[2].wait()
    q_hooks = {
        0: [(q_after_z, c)],
        1: [(q_after_z, d)],
        2: [(q_ready, b)],
        5: [(q_ready, c)],
        8: [(q_ready, d)],
    }
    stages = [step_a, step_b, step_c, step_d]

    def turn(i, carry):
        @pl.when(i < units)
        def _():
            k, r = head_of(i), i % thirds

            @pl.when(r == 0)
            def _():
                tail(k)

            prompt(i, k, r)

        for late in reversed(range(len(stages))):

            @pl.when((i >= late) & (i < units + late))
            def _(late=late):
                stages[late](i - late)

        for at_turn, calls in q_hooks.items():

            @pl.when(i == at_turn)
            def _(calls=calls):
                for call, at_k in calls:
                    call(at_k)

        return carry

    lax.fori_loop(0, units + len(stages) - 1, turn, 0)
    swap().start()
    swap().wait()
    out[...] = (total[pl.ds(2 * head, 2)] + x_part[...]).reshape(out.shape)


def fused(queries, prompt_keys, prompt_values, suffix_keys, suffix_values, suffix_lengths, slot_of_sample, out_weight):
    slots, heads, width = queries.shape
    kv = prompt_keys.shape[1]
    group = heads // kv
    rows = slots * group
    positions = prompt_keys.shape[0]
    samples = slot_of_sample.shape[0]
    columns = samples * group
    chunk = YS * CS * rows
    lanes = 128
    thirds = chunk // lanes
    units = kv * thirds
    tail_len = suffix_keys.shape[2]
    half, out_columns = samples // 2, out_weight.shape[1]
    unit = math.log2(math.e) / math.sqrt(width)

    flat_keys = prompt_keys.reshape(positions * kv, width)
    flat_values = prompt_values.reshape(positions * kv, width)

    bf16, f32 = jnp.bfloat16, jnp.float32
    vmem, hbm = pl.BlockSpec(memory_space=pltpu.VMEM), pl.BlockSpec(memory_space=pl.ANY)
    sem = pltpu.SemaphoreType.DMA
    return pl.pallas_call(
        functools.partial(kernel, unit),
        out_shape=jax.ShapeDtypeStruct((half, out_columns), f32),
        in_specs=[vmem, hbm, hbm, hbm, hbm, pl.BlockSpec(memory_space=pltpu.SMEM), vmem, hbm],
        out_specs=vmem,
        scratch_shapes=[
            pltpu.VMEM((kv, rows, width), bf16),
            pltpu.VMEM(flat_keys.shape, bf16),
            pltpu.VMEM(flat_values.shape, bf16),
            pltpu.VMEM((lanes, lanes), bf16),
            pltpu.VMEM((rows, columns), bf16),
            pltpu.VMEM((kv, ZS, chunk, width), bf16),
            pltpu.VMEM((kv, positions, width), bf16),
            pltpu.VMEM((kv, width + 16, positions), bf16),
            pltpu.VMEM((kv, slots, tail_len, width), bf16),
            pltpu.VMEM((kv, slots, tail_len, width), bf16),
            pltpu.VMEM(out_weight.shape[::-1], bf16),
            pltpu.VMEM((rows, width), f32),
            pltpu.VMEM((rows, tail_len), f32),
            pltpu.VMEM((rows, width), f32),
            pltpu.VMEM((thirds, ZS, width, lanes), f32),
            pltpu.VMEM((thirds, ZS, 8, lanes), f32),
            pltpu.VMEM((units, YS, CS, width, lanes), bf16),
            pltpu.VMEM((units, YS, CS, 8, lanes), f32),
            pltpu.VMEM((units, YS * CS - 1, width, lanes), bf16),
            pltpu.VMEM((units, YS * CS - 1, 8, lanes), f32),
            pltpu.VMEM((units, width, lanes), f32),
            pltpu.VMEM((units, width, lanes), bf16),
            pltpu.VMEM((units, 8, lanes), f32),
            pltpu.VMEM((units, ZS - 1, width, lanes), bf16),
            pltpu.VMEM((units, ZS - 1, 8, lanes), f32),
            pltpu.VMEM((units, YS, CS, group, lanes // group, width), bf16),
            pltpu.VMEM((ZS, samples // ZS, out_columns), f32),
            pltpu.VMEM((2, samples // ZS, out_columns), f32),
            sem((3,)),
            sem((kv, 2)),
            sem((kv, ZS - 1, 2)),
            sem((kv, YS * CS - 1, 2)),
            sem((units, YS * CS - 1, 4)),
            sem((units, ZS - 1, 4)),
            sem((units, YS * CS - 1, 2)),
            sem((2,)),
        ],
        compiler_params=pltpu.CompilerParams(
            collective_id=0, has_side_effects=True, vmem_limit_bytes=62 * 1024 * 1024
        ),
    )(
        queries,
        flat_keys,
        flat_values,
        suffix_keys,
        suffix_values,
        suffix_lengths,
        slot_of_sample.reshape(1, samples),
        out_weight.T,
    )


def partial_softmax(scores, values_block, equation):
    row_max = jnp.max(scores, axis=-1)
    weights = jnp.exp(scores - row_max[..., None])
    row_total = jnp.sum(weights, axis=-1)
    output = jnp.einsum(
        equation, weights.astype(jnp.bfloat16), values_block, preferred_element_type=jnp.float32
    )
    return (output, row_max, row_total)


def per_device(
    queries,
    prompt_keys,
    prompt_values,
    suffix_keys,
    suffix_values,
    suffix_lengths,
    slot_of_sample,
    out_weight,
):
    local_count, heads_local, head_width = queries.shape
    kv_local = prompt_keys.shape[1]
    group_size = heads_local // kv_local
    score_scale = 1.0 / math.sqrt(head_width)
    all_queries = lax.all_gather(queries, "seq", axis=0, tiled=True)
    total_rows = all_queries.shape[0]
    block_rows = math.gcd(total_rows, 64)

    def prefix_block(query_block):
        grouped = query_block.reshape(block_rows, kv_local, group_size, head_width)
        scores = (
            jnp.einsum("bkgd,pkd->bkgp", grouped, prompt_keys, preferred_element_type=jnp.float32)
            * score_scale
        )
        output, row_max, row_total = partial_softmax(scores, prompt_values, "bkgp,pkd->bkgd")
        return (
            output.reshape(block_rows, heads_local, head_width),
            row_max.reshape(block_rows, heads_local),
            row_total.reshape(block_rows, heads_local),
        )

    blocks = all_queries.reshape(total_rows // block_rows, block_rows, heads_local, head_width)
    pre_out, pre_max, pre_total = lax.map(prefix_block, blocks)
    pre_out = pre_out.reshape(total_rows, heads_local, head_width)
    pre_max = pre_max.reshape(total_rows, heads_local)
    pre_total = pre_total.reshape(total_rows, heads_local)
    my_slots = lax.axis_index("seq") * local_count + jnp.arange(local_count, dtype=jnp.int32)
    matches = (slot_of_sample[None, :] == my_slots[:, None]).astype(jnp.int32)
    samples = jnp.sum(matches * jnp.arange(total_rows, dtype=jnp.int32)[None, :], axis=1)
    own_queries = all_queries[samples].reshape(local_count, kv_local, group_size, head_width)
    tail_scores = (
        jnp.einsum("bkgd,bksd->bkgs", own_queries, suffix_keys, preferred_element_type=jnp.float32)
        * score_scale
    )
    positions = jnp.arange(suffix_keys.shape[2], dtype=jnp.int32)
    live_mask = positions[None, None, None, :] < suffix_lengths[:, None, None, None]
    tail_scores = jnp.where(live_mask, tail_scores, jnp.float32(-1e30))
    tail_out, tail_max, tail_total = partial_softmax(tail_scores, suffix_values, "bkgs,bksd->bkgd")
    tail_out = tail_out.reshape(local_count, heads_local, head_width)
    tail_max = tail_max.reshape(local_count, heads_local)
    tail_total = tail_total.reshape(local_count, heads_local)
    old_max = pre_max[samples]
    joint_max = jnp.maximum(old_max, tail_max)
    old_factor = jnp.exp(old_max - joint_max)
    new_factor = jnp.exp(tail_max - joint_max)
    joint_out = pre_out[samples] * old_factor[..., None] + tail_out * new_factor[..., None]
    joint_total = pre_total[samples] * old_factor + tail_total * new_factor
    pre_out = pre_out.at[samples].set(joint_out)
    pre_max = pre_max.at[samples].set(joint_max)
    pre_total = pre_total.at[samples].set(joint_total)
    got_out, got_max, got_total = (
        lax.all_to_all(pre_out[None], "seq", split_axis=1, concat_axis=0, tiled=True),
        lax.all_to_all(pre_max[None], "seq", split_axis=1, concat_axis=0, tiled=True),
        lax.all_to_all(pre_total[None], "seq", split_axis=1, concat_axis=0, tiled=True),
    )
    best = jnp.max(got_max, axis=0)
    factors = jnp.exp(got_max - best[None])
    merged_out = jnp.sum(got_out * factors[..., None], axis=0)
    merged_total = jnp.sum(got_total * factors, axis=0)
    attention = (merged_out / merged_total[..., None]).astype(jnp.bfloat16)
    attention = attention.reshape(local_count, heads_local * head_width)
    terms = jnp.dot(
        lax.all_gather(attention, "seq", axis=0, tiled=True),
        out_weight,
        preferred_element_type=jnp.float32,
    )
    return lax.psum_scatter(terms, "head", scatter_dimension=0, tiled=True)


def solution(mesh):
    placed = (
        P("seq", "head", None),
        P("seq", "head", None),
        P("seq", "head", None),
        P("seq", "head", None, None),
        P("seq", "head", None, None),
        P("seq"),
        P(),
        P("head", "seq"),
    )

    def body(*arrays):
        kv = arrays[1].shape[1]
        fits = mesh.shape["seq"] == ZS * YS * CS and mesh.shape["head"] == 2 and kv == ZS
        return (fused if fits else per_device)(*arrays)

    return jax.shard_map(body, mesh=mesh, in_specs=placed, out_specs=P("head", "seq"), check_vma=False)
```

```python
import functools
import math

import jax
import jax.numpy as jnp
from jax import lax
from jax.experimental import pallas as pl
from jax.experimental.pallas import tpu as pltpu
from jax.sharding import PartitionSpec as P

MESH = pl.DeviceIdType.MESH
NT = (((1,), (1,)), ((), ()))
TN = (((0,), (0,)), ((), ()))
NN = (((1,), (0,)), ((), ()))
LOW = -1e30
ZS, YS, CS = 4, 2, 2


def dot(a, b, dims):
    return lax.dot_general(a, b, dims, preferred_element_type=jnp.float32)


def merge(parts, unit):
    top = functools.reduce(jnp.maximum, [part[1] for part in parts])
    out, total = None, None
    for part_out, part_top, part_total in parts:
        factor = jnp.exp2((part_top - top) * unit)
        scaled, count = part_out * factor, part_total * factor
        out = scaled if out is None else out + scaled
        total = count if total is None else total + count
    return out, top, total


def kernel(
    unit,
    q_in,
    keys_in,
    values_in,
    tail_keys_in,
    tail_values_in,
    lengths,
    slot_of,
    weight_in,
    out,
    q_own,
    raw_keys,
    raw_values,
    perm,
    match,
    q_all,
    keys,
    values,
    tail_keys,
    tail_values,
    weight,
    own_q,
    tail_scores,
    tail_rows,
    tail_out,
    tail_stat,
    part,
    stat,
    core_part,
    core_stat,
    y_own,
    y_send,
    y_part,
    y_own_stat,
    y_send_stat,
    y_stat,
    z_send,
    z_send_stat,
    z_part,
    z_stat,
    att,
    total,
    x_part,
    load_sem,
    tail_sem,
    q_sems,
    qz_send_sem,
    qz_recv_sem,
    core_sems,
    y_sems,
    zs_send,
    zs_recv,
    zo_sems,
    az_send,
    az_recv,
    a_sems,
    x_sems,
):
    kv_count, rows_local, width = q_own.shape
    slots = lengths.shape[0]
    group = rows_local // slots
    samples = slot_of.shape[1]
    chunk = YS * CS * rows_local
    seq, head = lax.axis_index("seq"), lax.axis_index("head")
    z, y, core = seq // (YS * CS), (seq // CS) % YS, seq % CS
    other_y, other_core, other_head = 1 - y, 1 - core, 1 - head

    def at(z_to, y_to, core_to):
        return ((z_to * YS + y_to) * CS + core_to, head)

    z_peers = [at((z + step) % ZS, y, core) for step in range(1, ZS)]
    y_peer, core_peer, x_peer = at(z, other_y, core), at(z, y, other_core), (seq, other_head)
    order = [(3 * turn) % kv_count for turn in range(kv_count)]

    def remote(source, target, send, recv, device):
        return pltpu.make_async_remote_copy(
            src_ref=source, dst_ref=target, send_sem=send, recv_sem=recv, device_id=device, device_id_type=MESH
        )

    loads = [
        pltpu.make_async_copy(keys_in, raw_keys, load_sem.at[0]),
        pltpu.make_async_copy(values_in, raw_values, load_sem.at[1]),
        pltpu.make_async_copy(weight_in, weight, load_sem.at[2]),
    ]

    def tail_loads(k):
        return [
            pltpu.make_async_copy(tail_keys_in.at[:, k], tail_keys.at[k], tail_sem.at[k, 0]),
            pltpu.make_async_copy(tail_values_in.at[:, k], tail_values.at[k], tail_sem.at[k, 1]),
        ]

    loads[0].start()
    loads[1].start()
    for k in order:
        for load in tail_loads(k):
            load.start()
    loads[2].start()

    def grid(shape, axis):
        return lax.broadcasted_iota(jnp.int32, shape, axis)

    def onehot(chosen):
        return jnp.where(chosen, 1.0, 0.0).astype(jnp.bfloat16)

    flat = q_in[...].reshape(-1, width)
    shape = (rows_local, flat.shape[0])
    place = (grid(shape, 0) // group) * (kv_count * group) + grid(shape, 0) % group
    for k in order:
        q_own[k] = dot(onehot(grid(shape, 1) == place + k * group), flat, NN).astype(jnp.bfloat16)

    barrier = pltpu.get_barrier_semaphore()
    peers = z_peers + [y_peer, core_peer, x_peer]
    for peer in peers:
        pl.semaphore_signal(barrier, inc=1, device_id=peer, device_id_type=MESH)
    pl.semaphore_wait(barrier, len(peers))

    def q_z(k):
        return [
            remote(q_own.at[k], q_all.at[k, z, y, core], qz_send_sem.at[k, i], qz_recv_sem.at[k, i], z_peers[i])
            for i in range(ZS - 1)
        ]

    def q_y(k):
        mine = q_all.at[k, :, y, core]
        return remote(mine, mine, q_sems.at[k, 0], q_sems.at[k, 1], y_peer)

    def q_core(k):
        mine = q_all.at[k, :, :, core]
        return remote(mine, mine, q_sems.at[k, 2], q_sems.at[k, 3], core_peer)

    def q_start(k):
        for copy in q_z(k):
            copy.start()

    q_start(order[0])
    for k in order:
        q_all[k, z, y, core] = q_own[k]

    def q_after_z(k):
        for copy in q_z(k):
            copy.wait()
        q_y(k).start()

    def q_after_y(k):
        q_y(k).wait()
        q_core(k).start()

    def q_ready(k):
        q_core(k).wait()

    def split_keys():
        size = 256 // kv_count
        shape = (256, 256)
        pick = onehot(grid(shape, 1) == (grid(shape, 0) % size) * kv_count + grid(shape, 0) // size)

        def one(i, carry):
            rows = raw_keys[pl.ds(pl.multiple_of(i * 256, 256), 256), :]
            apart = dot(pick, rows, NN).astype(jnp.bfloat16)
            for k in range(kv_count):
                keys[k, pl.ds(pl.multiple_of(i * size, size), size), :] = apart[k * size : (k + 1) * size]
            return carry

        lax.fori_loop(0, raw_keys.shape[0] // 256, one, 0, unroll=4)

    def split_values():
        wide = 128 * kv_count
        shape = (wide, wide)
        pick = onehot(grid(shape, 0) == (grid(shape, 1) % 128) * kv_count + grid(shape, 1) // 128)

        def one(i, carry):
            rows = raw_values[pl.ds(pl.multiple_of(i * wide, wide), wide), :]
            apart = dot(rows, pick, TN).astype(jnp.bfloat16)
            for k in range(kv_count):
                values[k, :width, pl.ds(pl.multiple_of(i * 128, 128), 128)] = apart[:, k * 128 : (k + 1) * 128]
            return carry

        lax.fori_loop(0, raw_values.shape[0] // wide, one, 0, unroll=2)
        for k in range(kv_count):
            values[k, width:, :] = jnp.ones((values.shape[1] - width, values.shape[2]), jnp.bfloat16)

    def prepare():
        columns = samples * group
        row_slot = seq * slots + grid((rows_local, samples), 0) // group
        shape = (samples, columns)
        spread = onehot(grid(shape, 1) // group == grid(shape, 0))
        wide = dot(onehot(slot_of[...] == row_slot), spread, NN)
        shape = (rows_local, columns)
        match[...] = jnp.where(grid(shape, 1) % group == grid(shape, 0) % group, wide, 0.0).astype(jnp.bfloat16)
        shape = (group, chunk // group, chunk)
        perm[...] = onehot(grid(shape, 2) == grid(shape, 1) * group + grid(shape, 0)).reshape(chunk, chunk)

    def tail(k):
        for load in tail_loads(k):
            load.wait()
        every = q_all[k].reshape(samples * group, width)
        own_q[...] = dot(match[...], every, NN)
        for t in range(slots):
            rows = slice(t * group, (t + 1) * group)
            scores = dot(own_q[rows, :].astype(jnp.bfloat16), tail_keys[k, t], NT)
            tail_scores[rows, :] = jnp.where(grid(scores.shape, 1) < lengths[t], scores, LOW)
        scores = tail_scores[...]
        top = jnp.max(scores, axis=1, keepdims=True)
        weights = jnp.exp2((scores - top) * unit)
        count = jnp.sum(weights, axis=1, keepdims=True)
        tail_scores[...] = weights
        for t in range(slots):
            rows = slice(t * group, (t + 1) * group)
            tail_rows[rows, :] = dot(tail_scores[rows, :].astype(jnp.bfloat16), tail_values[k, t], NN)
        for c in range(samples * group // chunk):
            place = match[:, c * chunk : (c + 1) * chunk]
            here = place.astype(jnp.float32) > 0.5
            tail_out[c] = dot(tail_rows[...].astype(jnp.bfloat16), place, TN)
            tail_stat[c, 0:1] = jnp.max(jnp.where(here, top, LOW), axis=0, keepdims=True)
            tail_stat[c, 1:2] = jnp.sum(jnp.where(here, count, 0.0), axis=0, keepdims=True)

    def prompt(k, pair):
        q = q_all[k, pl.ds(pair * 2, 2)].reshape(2 * chunk, width)
        wide = 256
        count = 2 * chunk // wide
        scores = [dot(keys[k], q[:wide], NT)]
        tops, boths = [], []
        for j in range(count):
            if j + 1 < count:
                scores.append(dot(keys[k], q[(j + 1) * wide : (j + 2) * wide], NT))
            top = jnp.max(scores[j], axis=0, keepdims=True)
            weights = jnp.exp2((scores[j] - top) * unit).astype(jnp.bfloat16)
            tops.append(top)
            boths.append(dot(values[k], weights, NN))
        top, both = jnp.concatenate(tops, axis=1), jnp.concatenate(boths, axis=1)
        rows, count = both[:width], both[width : width + 1]
        for c in range(2):
            span = slice(c * chunk, (c + 1) * chunk)
            at_chunk = pair * 2 + c
            o, m, l = merge(
                [
                    (rows[:, span], top[:, span], count[:, span]),
                    (tail_out[at_chunk], tail_stat[at_chunk, 0:1], tail_stat[at_chunk, 1:2]),
                ],
                unit,
            )
            part[k, pair, c] = o.astype(jnp.bfloat16)
            stat[k, pair, c, 0:1] = m
            stat[k, pair, c, 1:2] = l

    def sum_core(k):
        return [
            remote(part.at[k, :, other_core], core_part.at[k], core_sems.at[k, 0], core_sems.at[k, 1], core_peer),
            remote(stat.at[k, :, other_core], core_stat.at[k], core_sems.at[k, 2], core_sems.at[k, 3], core_peer),
        ]

    def sum_y(k):
        return [
            remote(y_send.at[k], y_part.at[k], y_sems.at[k, 0], y_sems.at[k, 1], y_peer),
            remote(y_send_stat.at[k], y_stat.at[k], y_sems.at[k, 2], y_sems.at[k, 3], y_peer),
        ]

    def sum_z(k):
        slot = (z - k + ZS - 1) % ZS
        return [
            remote(z_send.at[k], z_part.at[slot], zs_send.at[k, 0], zs_recv.at[slot, 0], at(k, y, core)),
            remote(z_send_stat.at[k], z_stat.at[slot], zs_send.at[k, 1], zs_recv.at[slot, 1], at(k, y, core)),
        ]

    def att_z(k):
        mine = att.at[k, y, core]
        return [
            remote(mine, mine, az_send.at[i], az_recv.at[k], at((k + 1 + i) % ZS, y, core)) for i in range(ZS - 1)
        ]

    def att_y(k):
        mine = att.at[k, y, core]
        return remote(mine, mine, a_sems.at[k, 0], a_sems.at[k, 1], y_peer)

    def att_core(k):
        mine = att.at[k, :, core]
        return remote(mine, mine, a_sems.at[k, 2], a_sems.at[k, 3], core_peer)

    def step_a(k):
        for copy in sum_core(k):
            copy.start()

    def step_b(k):
        for copy in sum_core(k):
            copy.wait()

        def joined(i):
            return merge(
                [
                    (part[k, i, core].astype(jnp.float32), stat[k, i, core, 0:1], stat[k, i, core, 1:2]),
                    (core_part[k, i].astype(jnp.float32), core_stat[k, i, 0:1], core_stat[k, i, 1:2]),
                ],
                unit,
            )

        o, m, l = joined(other_y)
        y_send[k] = o.astype(jnp.bfloat16)
        y_send_stat[k, 0:1] = m
        y_send_stat[k, 1:2] = l
        for copy in sum_y(k):
            copy.start()
        o, m, l = joined(y)
        y_own[k] = o
        y_own_stat[k, 0:1] = m
        y_own_stat[k, 1:2] = l

    def step_c(k):
        for copy in sum_y(k):
            copy.wait()
        o, m, l = merge(
            [
                (y_own[k], y_own_stat[k, 0:1], y_own_stat[k, 1:2]),
                (y_part[k].astype(jnp.float32), y_stat[k, 0:1], y_stat[k, 1:2]),
            ],
            unit,
        )
        y_own[k] = o
        z_send[k] = o.astype(jnp.bfloat16)
        z_send_stat[k, 0:1] = m
        z_send_stat[k, 1:2] = l

        @pl.when(z != k)
        def _():
            for copy in sum_z(k):
                copy.start()

    def step_d(k):
        @pl.when(z != k)
        def _():
            for copy in sum_z(k):
                copy.wait_send()

        @pl.when(z == k)
        def _():
            parts = [(y_own[k], z_send_stat[k, 0:1], z_send_stat[k, 1:2])]
            for slot in range(ZS - 1):
                device = at(k, y, core)
                remote(z_send.at[k], z_part.at[slot], zs_send.at[k, 0], zs_recv.at[slot, 0], device).wait_recv()
                remote(z_send_stat.at[k], z_stat.at[slot], zs_send.at[k, 1], zs_recv.at[slot, 1], device).wait_recv()
                parts.append((z_part[slot].astype(jnp.float32), z_stat[slot, 0:1], z_stat[slot, 1:2]))
            o, _, l = merge(parts, unit)
            attention = (o / l).astype(jnp.bfloat16)
            rows = dot(perm[...], attention, NT).astype(jnp.bfloat16)
            att[k, y, core] = rows.reshape(att.shape[3:])
            for copy in att_z(k):
                copy.start()

    def step_e(k):
        @pl.when(z != k)
        def _():
            att_z(k)[0].wait_recv()

        att_y(k).start()

    def step_f(k):
        @pl.when(z == k)
        def _():
            for copy in att_z(k):
                copy.wait_send()

        att_y(k).wait()
        att_core(k).start()

    def step_g(k):
        att_core(k).wait()
        value = None
        for g in range(0, group, 2):
            block = jnp.concatenate(
                [
                    jnp.concatenate([att[k, i, j, g + h] for i in range(YS) for j in range(CS)], axis=0)
                    for h in range(2)
                ],
                axis=1,
            )
            first = (k * group + g) * width
            term = dot(block, weight[:, first : first + 2 * width], NT)
            value = term if value is None else value + term
        half = value.shape[0] // 2
        total[0] += value[:half]
        total[1] += value[half:]

    a, b, c, d = order
    prepare()
    loads[0].wait()
    split_keys()
    q_after_z(a)
    q_start(b)
    loads[1].wait()
    split_values()
    q_after_y(a)
    q_start(c)
    q_start(d)
    loads[2].wait()
    total[...] = jnp.zeros_like(total)
    q_ready(a)

    mid_hooks = {
        0: [(q_after_z, b)],
        2: [(step_b, a), (q_after_y, c)],
        4: [(step_e, a), (step_b, b)],
        6: [(step_e, b), (step_b, c)],
    }
    hooks = {
        0: [(q_after_y, b), (q_after_z, c)],
        1: [(step_a, a), (q_ready, b), (q_after_z, d)],
        2: [(step_c, a), (q_after_y, d)],
        3: [(step_d, a), (step_a, b), (q_ready, c)],
        4: [(step_f, a), (step_c, b)],
        5: [(step_a, c), (step_g, a), (step_d, b), (q_ready, d)],
        6: [(step_f, b), (step_c, c)],
        7: [(step_a, d), (step_g, b), (step_d, c)],
    }

    def run(i, table):
        for at_turn, calls in table.items():

            @pl.when(i == at_turn)
            def _(calls=calls):
                for call, at_k in calls:
                    call(at_k)

    def turn(i, carry):
        k, pair = (3 * (i // 2)) % kv_count, i % 2

        @pl.when(pair == 0)
        def _():
            tail(k)
            run(i, mid_hooks)

        prompt(k, pair)
        run(i, hooks)
        return carry

    lax.fori_loop(0, 2 * kv_count, turn, 0)
    step_b(d)
    step_e(c)
    step_c(d)
    step_f(c)
    step_d(d)
    step_g(c)
    step_e(d)
    step_f(d)
    step_g(d)
    swap = remote(total.at[other_head], x_part, x_sems.at[0], x_sems.at[1], x_peer)
    swap.start()
    swap.wait()
    out[...] = total[head] + x_part[...]


def fused(queries, prompt_keys, prompt_values, suffix_keys, suffix_values, suffix_lengths, slot_of_sample, out_weight):
    slots, heads, width = queries.shape
    kv = prompt_keys.shape[1]
    group = heads // kv
    rows = slots * group
    positions = prompt_keys.shape[0]
    samples = slot_of_sample.shape[0]
    columns = samples * group
    chunk = YS * CS * rows
    share = chunk // group
    tail_len = suffix_keys.shape[2]
    half, out_columns = samples // 2, out_weight.shape[1]
    unit = math.log2(math.e) / math.sqrt(width)

    flat_keys = prompt_keys.reshape(positions * kv, width)
    flat_values = prompt_values.reshape(positions * kv, width)

    bf16, f32 = jnp.bfloat16, jnp.float32
    vmem, hbm = pl.BlockSpec(memory_space=pltpu.VMEM), pl.BlockSpec(memory_space=pl.ANY)
    sem = pltpu.SemaphoreType.DMA
    return pl.pallas_call(
        functools.partial(kernel, unit),
        out_shape=jax.ShapeDtypeStruct((half, out_columns), f32),
        in_specs=[vmem, hbm, hbm, hbm, hbm, pl.BlockSpec(memory_space=pltpu.SMEM), vmem, hbm],
        out_specs=vmem,
        scratch_shapes=[
            pltpu.VMEM((kv, rows, width), bf16),
            pltpu.VMEM(flat_keys.shape, bf16),
            pltpu.VMEM(flat_values.shape, bf16),
            pltpu.VMEM((chunk, chunk), bf16),
            pltpu.VMEM((rows, columns), bf16),
            pltpu.VMEM((kv, ZS, YS, CS, rows, width), bf16),
            pltpu.VMEM((kv, positions, width), bf16),
            pltpu.VMEM((kv, width + 16, positions), bf16),
            pltpu.VMEM((kv, slots, tail_len, width), bf16),
            pltpu.VMEM((kv, slots, tail_len, width), bf16),
            pltpu.VMEM(out_weight.shape[::-1], bf16),
            pltpu.VMEM((rows, width), f32),
            pltpu.VMEM((rows, tail_len), f32),
            pltpu.VMEM((rows, width), f32),
            pltpu.VMEM((ZS, width, chunk), f32),
            pltpu.VMEM((ZS, 8, chunk), f32),
            pltpu.VMEM((kv, YS, CS, width, chunk), bf16),
            pltpu.VMEM((kv, YS, CS, 8, chunk), f32),
            pltpu.VMEM((kv, YS, width, chunk), bf16),
            pltpu.VMEM((kv, YS, 8, chunk), f32),
            pltpu.VMEM((kv, width, chunk), f32),
            pltpu.VMEM((kv, width, chunk), bf16),
            pltpu.VMEM((kv, width, chunk), bf16),
            pltpu.VMEM((kv, 8, chunk), f32),
            pltpu.VMEM((kv, 8, chunk), f32),
            pltpu.VMEM((kv, 8, chunk), f32),
            pltpu.VMEM((kv, width, chunk), bf16),
            pltpu.VMEM((kv, 8, chunk), f32),
            pltpu.VMEM((ZS - 1, width, chunk), bf16),
            pltpu.VMEM((ZS - 1, 8, chunk), f32),
            pltpu.VMEM((kv, YS, CS, group, share, width), bf16),
            pltpu.VMEM((2, half, out_columns), f32),
            pltpu.VMEM((half, out_columns), f32),
            sem((3,)),
            sem((kv, 2)),
            sem((kv, 4)),
            sem((kv, ZS - 1)),
            sem((kv, ZS - 1)),
            sem((kv, 4)),
            sem((kv, 4)),
            sem((kv, 2)),
            sem((ZS - 1, 2)),
            sem((1,)),
            sem((ZS - 1,)),
            sem((kv,)),
            sem((kv, 4)),
            sem((2,)),
        ],
        compiler_params=pltpu.CompilerParams(
            collective_id=0, has_side_effects=True, vmem_limit_bytes=62 * 1024 * 1024
        ),
    )(
        queries,
        flat_keys,
        flat_values,
        suffix_keys,
        suffix_values,
        suffix_lengths,
        slot_of_sample.reshape(1, samples),
        out_weight.T,
    )


def partial_softmax(scores, values_block, equation):
    row_max = jnp.max(scores, axis=-1)
    weights = jnp.exp(scores - row_max[..., None])
    row_total = jnp.sum(weights, axis=-1)
    output = jnp.einsum(
        equation, weights.astype(jnp.bfloat16), values_block, preferred_element_type=jnp.float32
    )
    return (output, row_max, row_total)


def per_device(
    queries,
    prompt_keys,
    prompt_values,
    suffix_keys,
    suffix_values,
    suffix_lengths,
    slot_of_sample,
    out_weight,
):
    local_count, heads_local, head_width = queries.shape
    kv_local = prompt_keys.shape[1]
    group_size = heads_local // kv_local
    score_scale = 1.0 / math.sqrt(head_width)
    all_queries = lax.all_gather(queries, "seq", axis=0, tiled=True)
    total_rows = all_queries.shape[0]
    block_rows = math.gcd(total_rows, 64)

    def prefix_block(query_block):
        grouped = query_block.reshape(block_rows, kv_local, group_size, head_width)
        scores = (
            jnp.einsum("bkgd,pkd->bkgp", grouped, prompt_keys, preferred_element_type=jnp.float32)
            * score_scale
        )
        output, row_max, row_total = partial_softmax(scores, prompt_values, "bkgp,pkd->bkgd")
        return (
            output.reshape(block_rows, heads_local, head_width),
            row_max.reshape(block_rows, heads_local),
            row_total.reshape(block_rows, heads_local),
        )

    blocks = all_queries.reshape(total_rows // block_rows, block_rows, heads_local, head_width)
    pre_out, pre_max, pre_total = lax.map(prefix_block, blocks)
    pre_out = pre_out.reshape(total_rows, heads_local, head_width)
    pre_max = pre_max.reshape(total_rows, heads_local)
    pre_total = pre_total.reshape(total_rows, heads_local)
    my_slots = lax.axis_index("seq") * local_count + jnp.arange(local_count, dtype=jnp.int32)
    matches = (slot_of_sample[None, :] == my_slots[:, None]).astype(jnp.int32)
    samples = jnp.sum(matches * jnp.arange(total_rows, dtype=jnp.int32)[None, :], axis=1)
    own_queries = all_queries[samples].reshape(local_count, kv_local, group_size, head_width)
    tail_scores = (
        jnp.einsum("bkgd,bksd->bkgs", own_queries, suffix_keys, preferred_element_type=jnp.float32)
        * score_scale
    )
    positions = jnp.arange(suffix_keys.shape[2], dtype=jnp.int32)
    live_mask = positions[None, None, None, :] < suffix_lengths[:, None, None, None]
    tail_scores = jnp.where(live_mask, tail_scores, jnp.float32(-1e30))
    tail_out, tail_max, tail_total = partial_softmax(tail_scores, suffix_values, "bkgs,bksd->bkgd")
    tail_out = tail_out.reshape(local_count, heads_local, head_width)
    tail_max = tail_max.reshape(local_count, heads_local)
    tail_total = tail_total.reshape(local_count, heads_local)
    old_max = pre_max[samples]
    joint_max = jnp.maximum(old_max, tail_max)
    old_factor = jnp.exp(old_max - joint_max)
    new_factor = jnp.exp(tail_max - joint_max)
    joint_out = pre_out[samples] * old_factor[..., None] + tail_out * new_factor[..., None]
    joint_total = pre_total[samples] * old_factor + tail_total * new_factor
    pre_out = pre_out.at[samples].set(joint_out)
    pre_max = pre_max.at[samples].set(joint_max)
    pre_total = pre_total.at[samples].set(joint_total)
    got_out, got_max, got_total = (
        lax.all_to_all(pre_out[None], "seq", split_axis=1, concat_axis=0, tiled=True),
        lax.all_to_all(pre_max[None], "seq", split_axis=1, concat_axis=0, tiled=True),
        lax.all_to_all(pre_total[None], "seq", split_axis=1, concat_axis=0, tiled=True),
    )
    best = jnp.max(got_max, axis=0)
    factors = jnp.exp(got_max - best[None])
    merged_out = jnp.sum(got_out * factors[..., None], axis=0)
    merged_total = jnp.sum(got_total * factors, axis=0)
    attention = (merged_out / merged_total[..., None]).astype(jnp.bfloat16)
    attention = attention.reshape(local_count, heads_local * head_width)
    terms = jnp.dot(
        lax.all_gather(attention, "seq", axis=0, tiled=True),
        out_weight,
        preferred_element_type=jnp.float32,
    )
    return lax.psum_scatter(terms, "head", scatter_dimension=0, tiled=True)


def solution(mesh):
    placed = (
        P("seq", "head", None),
        P("seq", "head", None),
        P("seq", "head", None),
        P("seq", "head", None, None),
        P("seq", "head", None, None),
        P("seq"),
        P(),
        P("head", "seq"),
    )

    def body(*arrays):
        kv = arrays[1].shape[1]
        fits = mesh.shape["seq"] == ZS * YS * CS and mesh.shape["head"] == 2 and kv == ZS
        return (fused if fits else per_device)(*arrays)

    return jax.shard_map(body, mesh=mesh, in_specs=placed, out_specs=P("head", "seq"), check_vma=False)
```

```python
import functools
import math

import jax
import jax.numpy as jnp
from jax import lax
from jax.experimental import pallas as pl
from jax.experimental.pallas import tpu as pltpu
from jax.sharding import PartitionSpec as P

MESH = pl.DeviceIdType.MESH
NT = (((1,), (1,)), ((), ()))
TN = (((0,), (0,)), ((), ()))
NN = (((1,), (0,)), ((), ()))
LOW = -1e30
ZS, YS, CS = 4, 2, 2


def dot(a, b, dims):
    return lax.dot_general(a, b, dims, preferred_element_type=jnp.float32)


def merge(parts, unit):
    top = functools.reduce(jnp.maximum, [part[1] for part in parts])
    out, total = None, None
    for part_out, part_top, part_total in parts:
        factor = jnp.exp2((part_top - top) * unit)
        scaled, count = part_out * factor, part_total * factor
        out = scaled if out is None else out + scaled
        total = count if total is None else total + count
    return out, top, total


def kernel(
    unit,
    q_in,
    keys_in,
    values_in,
    tail_keys_in,
    tail_values_in,
    lengths,
    slot_of,
    weight_in,
    out,
    q_own,
    raw_keys,
    raw_values,
    perm,
    match,
    q_all,
    keys,
    values,
    tail_keys,
    tail_values,
    weight,
    own_q,
    tail_scores,
    tail_rows,
    tail_out,
    tail_stat,
    part,
    stat,
    core_part,
    core_stat,
    y_own,
    y_send,
    y_part,
    y_own_stat,
    y_send_stat,
    y_stat,
    z_send,
    z_send_stat,
    z_part,
    z_stat,
    att,
    total,
    x_part,
    load_sem,
    tail_sem,
    q_sems,
    qz_send_sem,
    qz_recv_sem,
    core_sems,
    y_sems,
    zs_send,
    zs_recv,
    az_send,
    az_recv,
    a_sems,
    x_sems,
):
    kv_count, rows_local, width = q_own.shape
    slots = lengths.shape[0]
    group = rows_local // slots
    samples = slot_of.shape[1]
    chunk = YS * CS * rows_local
    lanes = part.shape[-1]
    thirds = chunk // lanes
    units = kv_count * thirds
    seq, head = lax.axis_index("seq"), lax.axis_index("head")
    z, y, core = seq // (YS * CS), (seq // CS) % YS, seq % CS
    other_y, other_core, other_head = 1 - y, 1 - core, 1 - head

    def at(z_to, y_to, core_to):
        return ((z_to * YS + y_to) * CS + core_to, head)

    z_peers = [at((z + step) % ZS, y, core) for step in range(1, ZS)]
    y_peer, core_peer, x_peer = at(z, other_y, core), at(z, y, other_core), (seq, other_head)
    order = [(3 * turn) % kv_count for turn in range(kv_count)]

    def remote(source, target, send, recv, device):
        return pltpu.make_async_remote_copy(
            src_ref=source, dst_ref=target, send_sem=send, recv_sem=recv, device_id=device, device_id_type=MESH
        )

    loads = [
        pltpu.make_async_copy(keys_in, raw_keys, load_sem.at[0]),
        pltpu.make_async_copy(values_in, raw_values, load_sem.at[1]),
        pltpu.make_async_copy(weight_in, weight, load_sem.at[2]),
    ]

    def tail_loads(k):
        return [
            pltpu.make_async_copy(tail_keys_in.at[:, k], tail_keys.at[k], tail_sem.at[k, 0]),
            pltpu.make_async_copy(tail_values_in.at[:, k], tail_values.at[k], tail_sem.at[k, 1]),
        ]

    loads[0].start()
    loads[1].start()
    for k in order:
        for load in tail_loads(k):
            load.start()
    loads[2].start()

    def grid(shape, axis):
        return lax.broadcasted_iota(jnp.int32, shape, axis)

    def onehot(chosen):
        return jnp.where(chosen, 1.0, 0.0).astype(jnp.bfloat16)

    flat = q_in[...].reshape(-1, width)
    shape = (rows_local, flat.shape[0])
    place = (grid(shape, 0) // group) * (kv_count * group) + grid(shape, 0) % group
    for k in order:
        q_own[k] = dot(onehot(grid(shape, 1) == place + k * group), flat, NN).astype(jnp.bfloat16)

    barrier = pltpu.get_barrier_semaphore()
    peers = z_peers + [y_peer, core_peer, x_peer]
    for peer in peers:
        pl.semaphore_signal(barrier, inc=1, device_id=peer, device_id_type=MESH)
    pl.semaphore_wait(barrier, len(peers))

    def block(y_of, core_of):
        return pl.ds((y_of * CS + core_of) * rows_local, rows_local)

    def q_z(k):
        return [
            remote(q_own.at[k], q_all.at[k, z, block(y, core)], qz_send_sem.at[k, i], qz_recv_sem.at[k, i], z_peers[i])
            for i in range(ZS - 1)
        ]

    def q_y(k):
        mine = q_all.at[k, :, block(y, core)]
        return remote(mine, mine, q_sems.at[k, 0], q_sems.at[k, 1], y_peer)

    def q_core(k):
        return [
            remote(
                q_all.at[k, :, block(i, core)],
                q_all.at[k, :, block(i, core)],
                q_sems.at[k, 2 + 2 * i],
                q_sems.at[k, 3 + 2 * i],
                core_peer,
            )
            for i in range(YS)
        ]

    for k in order:
        for copy in q_z(k):
            copy.start()
    for k in order:
        q_all[k, z, block(y, core), :] = q_own[k]

    def q_after_z(k):
        for copy in q_z(k):
            copy.wait()
        q_y(k).start()

    def q_after_y(k):
        q_y(k).wait()
        for copy in q_core(k):
            copy.start()

    def q_ready(k):
        for copy in q_core(k):
            copy.wait()

    def split_keys():
        size = 256 // kv_count
        shape = (256, 256)
        pick = onehot(grid(shape, 1) == (grid(shape, 0) % size) * kv_count + grid(shape, 0) // size)

        def one(i, carry):
            rows = raw_keys[pl.ds(pl.multiple_of(i * 256, 256), 256), :]
            apart = dot(pick, rows, NN).astype(jnp.bfloat16)
            for k in range(kv_count):
                keys[k, pl.ds(pl.multiple_of(i * size, size), size), :] = apart[k * size : (k + 1) * size]
            return carry

        lax.fori_loop(0, raw_keys.shape[0] // 256, one, 0, unroll=4)

    def split_values():
        wide = 128 * kv_count
        shape = (wide, wide)
        pick = onehot(grid(shape, 0) == (grid(shape, 1) % 128) * kv_count + grid(shape, 1) // 128)

        def one(i, carry):
            rows = raw_values[pl.ds(pl.multiple_of(i * wide, wide), wide), :]
            apart = dot(rows, pick, TN).astype(jnp.bfloat16)
            for k in range(kv_count):
                values[k, :width, pl.ds(pl.multiple_of(i * 128, 128), 128)] = apart[:, k * 128 : (k + 1) * 128]
            return carry

        lax.fori_loop(0, raw_values.shape[0] // wide, one, 0, unroll=2)
        for k in range(kv_count):
            values[k, width:, :] = jnp.ones((values.shape[1] - width, values.shape[2]), jnp.bfloat16)

    def prepare():
        columns = samples * group
        row_slot = seq * slots + grid((rows_local, samples), 0) // group
        shape = (samples, columns)
        spread = onehot(grid(shape, 1) // group == grid(shape, 0))
        wide = dot(onehot(slot_of[...] == row_slot), spread, NN)
        shape = (rows_local, columns)
        match[...] = jnp.where(grid(shape, 1) % group == grid(shape, 0) % group, wide, 0.0).astype(jnp.bfloat16)
        shape = (group, lanes // group, lanes)
        perm[...] = onehot(grid(shape, 2) == grid(shape, 1) * group + grid(shape, 0)).reshape(lanes, lanes)

    def tail(k):
        for load in tail_loads(k):
            load.wait()
        every = q_all[k].reshape(samples * group, width)
        own_q[...] = dot(match[...], every, NN)
        for t in range(slots):
            rows = slice(t * group, (t + 1) * group)
            scores = dot(own_q[rows, :].astype(jnp.bfloat16), tail_keys[k, t], NT)
            tail_scores[rows, :] = jnp.where(grid(scores.shape, 1) < lengths[t], scores, LOW)
        scores = tail_scores[...]
        top = jnp.max(scores, axis=1, keepdims=True)
        weights = jnp.exp2((scores - top) * unit)
        count = jnp.sum(weights, axis=1, keepdims=True)
        tail_scores[...] = weights
        for t in range(slots):
            rows = slice(t * group, (t + 1) * group)
            tail_rows[rows, :] = dot(tail_scores[rows, :].astype(jnp.bfloat16), tail_values[k, t], NN)
        for c in range(samples * group // chunk):
            place = match[:, c * chunk : (c + 1) * chunk]
            here = place.astype(jnp.float32) > 0.5
            rows = dot(tail_rows[...].astype(jnp.bfloat16), place, TN)
            best = jnp.max(jnp.where(here, top, LOW), axis=0, keepdims=True)
            sums = jnp.sum(jnp.where(here, count, 0.0), axis=0, keepdims=True)
            for r in range(thirds):
                span = slice(r * lanes, (r + 1) * lanes)
                tail_out[r, c] = rows[:, span]
                tail_stat[r, c, 0:1] = best[:, span]
                tail_stat[r, c, 1:2] = sums[:, span]

    def prompt(u, k, r):
        q = q_all[k, :, pl.ds(pl.multiple_of(r * lanes, lanes), lanes), :]
        scores = dot(keys[k], q.reshape(ZS * lanes, width), NT)
        top = jnp.max(scores, axis=0, keepdims=True)
        weights = jnp.exp2((scores - top) * unit).astype(jnp.bfloat16)
        both = dot(values[k], weights, NN)
        for c in range(ZS):
            span = slice(c * lanes, (c + 1) * lanes)
            o, m, l = merge(
                [
                    (both[:width, span], top[:, span], both[width : width + 1, span]),
                    (tail_out[r, c], tail_stat[r, c, 0:1], tail_stat[r, c, 1:2]),
                ],
                unit,
            )
            part[u, c // CS, c % CS] = o.astype(jnp.bfloat16)
            stat[u, c // CS, c % CS, 0:1] = m
            stat[u, c // CS, c % CS, 1:2] = l

    def sum_core(u):
        return [
            remote(part.at[u, :, other_core], core_part.at[u], core_sems.at[u, 0], core_sems.at[u, 1], core_peer),
            remote(stat.at[u, :, other_core], core_stat.at[u], core_sems.at[u, 2], core_sems.at[u, 3], core_peer),
        ]

    def sum_y(u):
        return [
            remote(y_send.at[u], y_part.at[u], y_sems.at[u, 0], y_sems.at[u, 1], y_peer),
            remote(y_send_stat.at[u], y_stat.at[u], y_sems.at[u, 2], y_sems.at[u, 3], y_peer),
        ]

    def head_of(u):
        return (3 * (u // thirds)) % kv_count

    def sum_z_out(u):
        k, r = head_of(u), u % thirds
        slot = (z - k + 2 * ZS - 1) % ZS
        return [
            remote(z_send.at[u], z_part.at[r, slot], zs_send.at[u, 0], zs_recv.at[r, slot, 0], at(k, y, core)),
            remote(z_send_stat.at[u], z_stat.at[r, slot], zs_send.at[u, 1], zs_recv.at[r, slot, 1], at(k, y, core)),
        ]

    def sum_z_in(u, slot):
        r = u % thirds
        return [
            remote(z_send.at[u], z_part.at[r, slot], zs_send.at[u, 0], zs_recv.at[r, slot, 0], y_peer),
            remote(z_send_stat.at[u], z_stat.at[r, slot], zs_send.at[u, 1], zs_recv.at[r, slot, 1], y_peer),
        ]

    def att_z(u, i):
        mine = att.at[u, y, core]
        return remote(mine, mine, az_send.at[u, i], az_recv.at[u], z_peers[i])

    def att_y(u):
        mine = att.at[u, y, core]
        return remote(mine, mine, a_sems.at[u, 0], a_sems.at[u, 1], y_peer)

    def att_core(u):
        mine = att.at[u, :, core]
        return remote(mine, mine, a_sems.at[u, 2], a_sems.at[u, 3], core_peer)

    def swap():
        return remote(total.at[pl.ds(2 * other_head, 2)], x_part, x_sems.at[0], x_sems.at[1], x_peer)

    def step_a(u):
        for copy in sum_core(u):
            copy.start()

    def step_b(u):
        for copy in sum_core(u):
            copy.wait()

        def joined(i):
            return merge(
                [
                    (part[u, i, core].astype(jnp.float32), stat[u, i, core, 0:1], stat[u, i, core, 1:2]),
                    (core_part[u, i].astype(jnp.float32), core_stat[u, i, 0:1], core_stat[u, i, 1:2]),
                ],
                unit,
            )

        o, m, l = joined(other_y)
        y_send[u] = o.astype(jnp.bfloat16)
        y_send_stat[u, 0:1] = m
        y_send_stat[u, 1:2] = l
        for copy in sum_y(u):
            copy.start()
        o, m, l = joined(y)
        y_own[u] = o
        y_own_stat[u, 0:1] = m
        y_own_stat[u, 1:2] = l

    def step_c(u):
        for copy in sum_y(u):
            copy.wait()
        o, m, l = merge(
            [
                (y_own[u], y_own_stat[u, 0:1], y_own_stat[u, 1:2]),
                (y_part[u].astype(jnp.float32), y_stat[u, 0:1], y_stat[u, 1:2]),
            ],
            unit,
        )
        y_own[u] = o
        z_send[u] = o.astype(jnp.bfloat16)
        z_send_stat[u, 0:1] = m
        z_send_stat[u, 1:2] = l

        @pl.when(z != head_of(u))
        def _():
            for copy in sum_z_out(u):
                copy.start()

    def step_d(u):
        @pl.when(z != head_of(u))
        def _():
            for copy in sum_z_out(u):
                copy.wait_send()

        @pl.when(z == head_of(u))
        def _():
            parts = [(y_own[u], z_send_stat[u, 0:1], z_send_stat[u, 1:2])]
            r = u % thirds
            for slot in range(ZS - 1):
                for copy in sum_z_in(u, slot):
                    copy.wait_recv()
                parts.append((z_part[r, slot].astype(jnp.float32), z_stat[r, slot, 0:1], z_stat[r, slot, 1:2]))
            o, _, l = merge(parts, unit)
            attention = (o / l).astype(jnp.bfloat16)
            rows = dot(perm[...], attention, NT).astype(jnp.bfloat16)
            att[u, y, core] = rows.reshape(att.shape[3:])
            for i in range(ZS - 1):
                att_z(u, i).start()

    def step_e(u):
        @pl.when(z != head_of(u))
        def _():
            att_z(u, 0).wait_recv()

        att_y(u).start()

    def step_f(u):
        @pl.when(z == head_of(u))
        def _():
            for i in range(ZS - 1):
                att_z(u, i).wait_send()

        att_y(u).wait()
        att_core(u).start()

    def step_g(u):
        att_core(u).wait()

        @pl.when(u % thirds == thirds - 1)
        def _():
            project(u // thirds)

    def project(turn_of):
        k = (3 * turn_of) % kv_count
        value = None
        for g in range(0, group, 2):
            rows = jnp.concatenate(
                [
                    jnp.concatenate(
                        [
                            att[turn_of * thirds + r, i, j, g + h]
                            for i in range(YS)
                            for j in range(CS)
                            for r in range(thirds)
                        ],
                        axis=0,
                    )
                    for h in range(2)
                ],
                axis=1,
            )
            first = pl.multiple_of((k * group + g) * width, 2 * width)
            term = dot(rows, weight[:, pl.ds(first, 2 * width)], NT)
            value = term if value is None else value + term
        total[...] += value.reshape(total.shape)

    a, b, c, d = order
    prepare()
    loads[0].wait()
    split_keys()
    q_after_z(a)
    loads[1].wait()
    split_values()
    q_after_y(a)
    q_after_z(b)
    q_ready(a)

    total[...] = jnp.zeros_like(total)
    loads[2].wait()
    q_hooks = {
        0: [(q_after_z, c), (q_after_y, b)],
        1: [(q_after_z, d)],
        2: [(q_ready, b), (q_after_y, c)],
        3: [(q_after_y, d)],
        5: [(q_ready, c)],
        8: [(q_ready, d)],
    }
    stages = [step_a, step_b, step_c, step_d, step_e, step_f, step_g]

    def turn(i, carry):
        @pl.when(i < units)
        def _():
            k, r = head_of(i), i % thirds

            @pl.when(r == 0)
            def _():
                tail(k)

            prompt(i, k, r)

        for late in reversed(range(len(stages))):

            @pl.when((i >= late) & (i < units + late))
            def _(late=late):
                stages[late](i - late)

        for at_turn, calls in q_hooks.items():

            @pl.when(i == at_turn)
            def _(calls=calls):
                for call, at_k in calls:
                    call(at_k)

        return carry

    lax.fori_loop(0, units + len(stages) - 1, turn, 0)
    swap().start()
    swap().wait()
    out[...] = (total[pl.ds(2 * head, 2)] + x_part[...]).reshape(out.shape)


def fused(queries, prompt_keys, prompt_values, suffix_keys, suffix_values, suffix_lengths, slot_of_sample, out_weight):
    slots, heads, width = queries.shape
    kv = prompt_keys.shape[1]
    group = heads // kv
    rows = slots * group
    positions = prompt_keys.shape[0]
    samples = slot_of_sample.shape[0]
    columns = samples * group
    chunk = YS * CS * rows
    lanes = 128
    thirds = chunk // lanes
    units = kv * thirds
    tail_len = suffix_keys.shape[2]
    half, out_columns = samples // 2, out_weight.shape[1]
    unit = math.log2(math.e) / math.sqrt(width)

    flat_keys = prompt_keys.reshape(positions * kv, width)
    flat_values = prompt_values.reshape(positions * kv, width)

    bf16, f32 = jnp.bfloat16, jnp.float32
    vmem, hbm = pl.BlockSpec(memory_space=pltpu.VMEM), pl.BlockSpec(memory_space=pl.ANY)
    sem = pltpu.SemaphoreType.DMA
    return pl.pallas_call(
        functools.partial(kernel, unit),
        out_shape=jax.ShapeDtypeStruct((half, out_columns), f32),
        in_specs=[vmem, hbm, hbm, hbm, hbm, pl.BlockSpec(memory_space=pltpu.SMEM), vmem, hbm],
        out_specs=vmem,
        scratch_shapes=[
            pltpu.VMEM((kv, rows, width), bf16),
            pltpu.VMEM(flat_keys.shape, bf16),
            pltpu.VMEM(flat_values.shape, bf16),
            pltpu.VMEM((lanes, lanes), bf16),
            pltpu.VMEM((rows, columns), bf16),
            pltpu.VMEM((kv, ZS, chunk, width), bf16),
            pltpu.VMEM((kv, positions, width), bf16),
            pltpu.VMEM((kv, width + 16, positions), bf16),
            pltpu.VMEM((kv, slots, tail_len, width), bf16),
            pltpu.VMEM((kv, slots, tail_len, width), bf16),
            pltpu.VMEM(out_weight.shape[::-1], bf16),
            pltpu.VMEM((rows, width), f32),
            pltpu.VMEM((rows, tail_len), f32),
            pltpu.VMEM((rows, width), f32),
            pltpu.VMEM((thirds, ZS, width, lanes), f32),
            pltpu.VMEM((thirds, ZS, 8, lanes), f32),
            pltpu.VMEM((units, YS, CS, width, lanes), bf16),
            pltpu.VMEM((units, YS, CS, 8, lanes), f32),
            pltpu.VMEM((units, YS, width, lanes), bf16),
            pltpu.VMEM((units, YS, 8, lanes), f32),
            pltpu.VMEM((units, width, lanes), f32),
            pltpu.VMEM((units, width, lanes), bf16),
            pltpu.VMEM((units, width, lanes), bf16),
            pltpu.VMEM((units, 8, lanes), f32),
            pltpu.VMEM((units, 8, lanes), f32),
            pltpu.VMEM((units, 8, lanes), f32),
            pltpu.VMEM((units, width, lanes), bf16),
            pltpu.VMEM((units, 8, lanes), f32),
            pltpu.VMEM((thirds, ZS - 1, width, lanes), bf16),
            pltpu.VMEM((thirds, ZS - 1, 8, lanes), f32),
            pltpu.VMEM((units, YS, CS, group, lanes // group, width), bf16),
            pltpu.VMEM((ZS, samples // ZS, out_columns), f32),
            pltpu.VMEM((2, samples // ZS, out_columns), f32),
            sem((3,)),
            sem((kv, 2)),
            sem((kv, 6)),
            sem((kv, ZS - 1)),
            sem((kv, ZS - 1)),
            sem((units, 4)),
            sem((units, 4)),
            sem((units, 2)),
            sem((thirds, ZS - 1, 2)),
            sem((units, ZS - 1)),
            sem((units,)),
            sem((units, 4)),
            sem((2,)),
        ],
        compiler_params=pltpu.CompilerParams(
            collective_id=0, has_side_effects=True, vmem_limit_bytes=62 * 1024 * 1024
        ),
    )(
        queries,
        flat_keys,
        flat_values,
        suffix_keys,
        suffix_values,
        suffix_lengths,
        slot_of_sample.reshape(1, samples),
        out_weight.T,
    )


def partial_softmax(scores, values_block, equation):
    row_max = jnp.max(scores, axis=-1)
    weights = jnp.exp(scores - row_max[..., None])
    row_total = jnp.sum(weights, axis=-1)
    output = jnp.einsum(
        equation, weights.astype(jnp.bfloat16), values_block, preferred_element_type=jnp.float32
    )
    return (output, row_max, row_total)


def per_device(
    queries,
    prompt_keys,
    prompt_values,
    suffix_keys,
    suffix_values,
    suffix_lengths,
    slot_of_sample,
    out_weight,
):
    local_count, heads_local, head_width = queries.shape
    kv_local = prompt_keys.shape[1]
    group_size = heads_local // kv_local
    score_scale = 1.0 / math.sqrt(head_width)
    all_queries = lax.all_gather(queries, "seq", axis=0, tiled=True)
    total_rows = all_queries.shape[0]
    block_rows = math.gcd(total_rows, 64)

    def prefix_block(query_block):
        grouped = query_block.reshape(block_rows, kv_local, group_size, head_width)
        scores = (
            jnp.einsum("bkgd,pkd->bkgp", grouped, prompt_keys, preferred_element_type=jnp.float32)
            * score_scale
        )
        output, row_max, row_total = partial_softmax(scores, prompt_values, "bkgp,pkd->bkgd")
        return (
            output.reshape(block_rows, heads_local, head_width),
            row_max.reshape(block_rows, heads_local),
            row_total.reshape(block_rows, heads_local),
        )

    blocks = all_queries.reshape(total_rows // block_rows, block_rows, heads_local, head_width)
    pre_out, pre_max, pre_total = lax.map(prefix_block, blocks)
    pre_out = pre_out.reshape(total_rows, heads_local, head_width)
    pre_max = pre_max.reshape(total_rows, heads_local)
    pre_total = pre_total.reshape(total_rows, heads_local)
    my_slots = lax.axis_index("seq") * local_count + jnp.arange(local_count, dtype=jnp.int32)
    matches = (slot_of_sample[None, :] == my_slots[:, None]).astype(jnp.int32)
    samples = jnp.sum(matches * jnp.arange(total_rows, dtype=jnp.int32)[None, :], axis=1)
    own_queries = all_queries[samples].reshape(local_count, kv_local, group_size, head_width)
    tail_scores = (
        jnp.einsum("bkgd,bksd->bkgs", own_queries, suffix_keys, preferred_element_type=jnp.float32)
        * score_scale
    )
    positions = jnp.arange(suffix_keys.shape[2], dtype=jnp.int32)
    live_mask = positions[None, None, None, :] < suffix_lengths[:, None, None, None]
    tail_scores = jnp.where(live_mask, tail_scores, jnp.float32(-1e30))
    tail_out, tail_max, tail_total = partial_softmax(tail_scores, suffix_values, "bkgs,bksd->bkgd")
    tail_out = tail_out.reshape(local_count, heads_local, head_width)
    tail_max = tail_max.reshape(local_count, heads_local)
    tail_total = tail_total.reshape(local_count, heads_local)
    old_max = pre_max[samples]
    joint_max = jnp.maximum(old_max, tail_max)
    old_factor = jnp.exp(old_max - joint_max)
    new_factor = jnp.exp(tail_max - joint_max)
    joint_out = pre_out[samples] * old_factor[..., None] + tail_out * new_factor[..., None]
    joint_total = pre_total[samples] * old_factor + tail_total * new_factor
    pre_out = pre_out.at[samples].set(joint_out)
    pre_max = pre_max.at[samples].set(joint_max)
    pre_total = pre_total.at[samples].set(joint_total)
    got_out, got_max, got_total = (
        lax.all_to_all(pre_out[None], "seq", split_axis=1, concat_axis=0, tiled=True),
        lax.all_to_all(pre_max[None], "seq", split_axis=1, concat_axis=0, tiled=True),
        lax.all_to_all(pre_total[None], "seq", split_axis=1, concat_axis=0, tiled=True),
    )
    best = jnp.max(got_max, axis=0)
    factors = jnp.exp(got_max - best[None])
    merged_out = jnp.sum(got_out * factors[..., None], axis=0)
    merged_total = jnp.sum(got_total * factors, axis=0)
    attention = (merged_out / merged_total[..., None]).astype(jnp.bfloat16)
    attention = attention.reshape(local_count, heads_local * head_width)
    terms = jnp.dot(
        lax.all_gather(attention, "seq", axis=0, tiled=True),
        out_weight,
        preferred_element_type=jnp.float32,
    )
    return lax.psum_scatter(terms, "head", scatter_dimension=0, tiled=True)


def solution(mesh):
    placed = (
        P("seq", "head", None),
        P("seq", "head", None),
        P("seq", "head", None),
        P("seq", "head", None, None),
        P("seq", "head", None, None),
        P("seq"),
        P(),
        P("head", "seq"),
    )

    def body(*arrays):
        kv = arrays[1].shape[1]
        fits = mesh.shape["seq"] == ZS * YS * CS and mesh.shape["head"] == 2 and kv == ZS
        return (fused if fits else per_device)(*arrays)

    return jax.shard_map(body, mesh=mesh, in_specs=placed, out_specs=P("head", "seq"), check_vma=False)
```
